128 devices in a mesh: section: 2 (over z_hi), ctx: 2 (over z_lo), fsdp: 32 (over y, x, core).
Axes of the slice: x: 4, y: 4, z: 4 (z_hi: 2, z_lo: 2; z = z_hi * 2 + z_lo), core: 2. Of those that a mesh axis runs over, the one named last changes fastest.
Arguments:
- inputs: bfloat16 [2, 32, 256, 1024], P(None, 'fsdp', 'ctx'), may hold values from -6 to 6
- cotangent: bfloat16 [2, 32, 256, 1024], P(None, 'fsdp', 'ctx'), may hold values from -6 to 6
- segments: int32 [2, 32, 256], P(None, 'fsdp'), may hold values from 0 to 3, as said below
- positions: int32 [2, 32, 256], P(None, 'fsdp', 'ctx'), may hold values from 0 to 767, as said below
- attention_gain: bfloat16 [2, 1024], P('section', 'fsdp'), may hold values from 0.5 to 1.5
- attention_bias: bfloat16 [2, 1024], P('section', 'fsdp'), may hold values from -2 to 2
- joint_weight: bfloat16 [2, 1024, 3072], P('section', 'fsdp'), may hold values from -0.1875 to 0.1875
- joint_bias: bfloat16 [2, 3072], P('section', 'fsdp'), may hold values from -2 to 2
- output_weight: bfloat16 [2, 1024, 1024], P('section', 'fsdp'), may hold values from -0.5 to 0.5
- output_bias: bfloat16 [2, 1024], P('section', 'fsdp'), may hold values from -2 to 2
- feed_gain: bfloat16 [2, 1024], P('section', 'fsdp'), may hold values from 0.5 to 1.5
- feed_bias: bfloat16 [2, 1024], P('section', 'fsdp'), may hold values from -2 to 2
- up_weight: bfloat16 [2, 1024, 4096], P('section', 'fsdp'), may hold values from -0.1875 to 0.1875
- up_bias: bfloat16 [2, 4096], P('section', 'fsdp'), may hold values from -2 to 2
- down_weight: bfloat16 [2, 4096, 1024], P('section', 'fsdp'), may hold values from -0.09375 to 0.09375
- down_bias: bfloat16 [2, 1024], P('section', 'fsdp'), may hold values from -2 to 2
Outputs:
- section_out: bfloat16 [2, 2, 32, 256, 1024], P('section', None, 'fsdp', 'ctx')
- input_grad: bfloat16 [2, 2, 32, 256, 1024], P('section', None, 'fsdp', 'ctx')
- attention_gain_grad: float32 [2, 1024], P('section', 'fsdp')
- attention_bias_grad: float32 [2, 1024], P('section', 'fsdp')
- joint_weight_grad: float32 [2, 1024, 3072], P('section', 'fsdp')
- joint_bias_grad: float32 [2, 3072], P('section', 'fsdp')
- output_weight_grad: float32 [2, 1024, 1024], P('section', 'fsdp')
- output_bias_grad: float32 [2, 1024], P('section', 'fsdp')
- feed_gain_grad: float32 [2, 1024], P('section', 'fsdp')
- feed_bias_grad: float32 [2, 1024], P('section', 'fsdp')
- up_weight_grad: float32 [2, 1024, 4096], P('section', 'fsdp')
- up_bias_grad: float32 [2, 4096], P('section', 'fsdp')
- down_weight_grad: float32 [2, 4096, 1024], P('section', 'fsdp')
- down_bias_grad: float32 [2, 1024], P('section', 'fsdp')
The draws below stay inside these ranges and needn't reach their ends.
Inputs may be any that keep to these rules, and one draw needn't show every extreme that they name: `segments`: document numbers of a sequence start at 0 and rise by one at each new document; every sequence has the same number of documents, and its last one carries the largest number allowed; one document of every sequence holds tokens 256 / 2 - 1 and 128. Within a document positions rise by one from token to token; the last token of every sequence has position 767.
All inputs are finite; a program needn't handle non-finite values.
Results may differ from the reference program's by a relative error of at most 0.024.
Values may be sent and summed in bfloat16 or wider, within the bound.
No kernel may reach another device: no remote copies, remote signals or barrier semaphores. Data moves between devices by JAX's collectives and lax.ppermute only.
A program may use at most 192 MiB of HBM per device.

```python
import math
import jax
import jax.numpy as jnp
from jax import lax

D = 1024
HEADS = 16
HEAD_DIM = 64
ROT = 16
FF = 4096
MB = 2
SEQ = 256
SEQS = 32
SECTIONS = 2


def documents(key):
    shape = (MB, SEQS, SEQ)
    number = max(1, min(3, SEQ // 64))
    index = jnp.arange(SEQ, dtype=jnp.int32)
    ranks = jax.random.randint(jax.random.fold_in(key, 11), shape, 0, 1 << 20) * SEQ + index
    barred = (index == 0) | (index == SEQ // 2)
    ranks = jnp.where(barred, jnp.int32(2147483647), ranks).astype(jnp.int32)
    lowest = -lax.top_k(-ranks, number)[0][..., number - 1:number]
    starts = (ranks <= lowest) & jnp.logical_not(barred)
    segment_ids = jnp.cumsum(starts.astype(jnp.int32), -1).astype(jnp.int32)
    begin = lax.cummax(jnp.where(starts, index, 0).astype(jnp.int32), axis=2)
    offsets = jax.random.randint(jax.random.fold_in(key, 12), shape, 0, 512)
    opening = jnp.take_along_axis(offsets, begin, axis=2)
    inside = (opening + index - begin).astype(jnp.int32)
    final = segment_ids == segment_ids[..., SEQ - 1:SEQ]
    return (segment_ids, jnp.where(final, index + 512, inside).astype(jnp.int32))


def draw_segments(key, part):
    shared = documents(key)
    return shared[0]


def draw_positions(key, part):
    shared = documents(key)
    return shared[1]


def levels(stream_key, dims, pieces, low, high):
    loudness = 1.0
    for dim, parts in pieces:
        steps = jax.random.uniform(jax.random.fold_in(jax.random.fold_in(stream_key, 6), dim), (parts,), jnp.float32, low / len(pieces), high / len(pieces))
        loudness = loudness * jnp.repeat(jnp.exp(steps), dims[dim] // parts).reshape((-1,) + (1,) * (len(dims) - 1 - dim))
    return loudness


def bell_draw(rng, shape, width, limit, shards=(), kind=jnp.bfloat16):
    result = width * jax.random.normal(rng, shape, jnp.float32)
    if shards:
        result = result * levels(rng, shape, shards, -0.22, 0.18)
    return jnp.clip(result, -limit, limit).astype(kind)


def setup_inputs(seed: int = 0) -> dict:
    key_list = jax.random.split(jax.random.key(seed), 17)
    inputs = bell_draw(key_list[0], (MB, SEQS, SEQ, D), 1.0, 6.0, ((1, 32), (2, 2)))
    cotangent = bell_draw(key_list[1], (MB, SEQS, SEQ, D), 1.0, 6.0, ((1, 32), (2, 2)))
    segments = draw_segments(jax.random.fold_in(key_list[16], 71), 0)
    positions = draw_positions(jax.random.fold_in(key_list[16], 71), 0)
    attention_gain = jnp.clip(1.0 + 0.1 * jax.random.normal(key_list[4], (SECTIONS, D), jnp.float32), 0.5, 1.5).astype(jnp.bfloat16)
    attention_bias = bell_draw(key_list[5], (SECTIONS, D), 0.3, 2.0, ((0, 2), (1, 32)))
    joint_weight = bell_draw(key_list[6], (SECTIONS, D, 3 * D), D ** -0.5, 0.1875, ((0, 2), (1, 32)))
    joint_bias = bell_draw(key_list[7], (SECTIONS, 3 * D), 0.3, 2.0, ((0, 2), (1, 32)))
    output_weight = bell_draw(key_list[8], (SECTIONS, D, D), (D // 8) ** -0.5, 0.5, ((0, 2), (1, 32)))
    output_bias = bell_draw(key_list[9], (SECTIONS, D), 0.3, 2.0, ((0, 2), (1, 32)))
    feed_gain = jnp.clip(1.0 + 0.1 * jax.random.normal(key_list[10], (SECTIONS, D), jnp.float32), 0.5, 1.5).astype(jnp.bfloat16)
    feed_bias = bell_draw(key_list[11], (SECTIONS, D), 0.3, 2.0, ((0, 2), (1, 32)))
    up_weight = bell_draw(key_list[12], (SECTIONS, D, FF), D ** -0.5, 0.1875, ((0, 2), (1, 32)))
    up_bias = bell_draw(key_list[13], (SECTIONS, FF), 0.3, 2.0, ((0, 2), (1, 32)))
    down_weight = bell_draw(key_list[14], (SECTIONS, FF, D), FF ** -0.5, 0.09375, ((0, 2), (1, 32)))
    down_bias = bell_draw(key_list[15], (SECTIONS, D), 0.3, 2.0, ((0, 2), (1, 32)))
    return {"inputs": inputs, "cotangent": cotangent, "segments": segments, "positions": positions, "attention_gain": attention_gain, "attention_bias": attention_bias, "joint_weight": joint_weight, "joint_bias": joint_bias, "output_weight": output_weight, "output_bias": output_bias, "feed_gain": feed_gain, "feed_bias": feed_bias, "up_weight": up_weight, "up_bias": up_bias, "down_weight": down_weight, "down_bias": down_bias}


@jax.custom_vjp
def low(v):
    return lax.optimization_barrier(v.astype(jnp.bfloat16)).astype(jnp.float32)

@jax.custom_vjp
def low_back(v):
    return v

def low_keep(v):
    return (low(v), None)

def low_pass(kept, grad):
    return (grad,)

def back_keep(v):
    return (v, None)

def back_low(kept, grad):
    return (low(grad),)
low.defvjp(low_keep, low_pass)
low_back.defvjp(back_keep, back_low)
HIGHEST = lax.Precision.HIGHEST

def layer_norm(values, gain, bias):
    centred = values - lax.optimization_barrier(jnp.mean(values, -1, keepdims=True))
    return centred * lax.rsqrt(lax.optimization_barrier(jnp.mean(centred * centred, -1, keepdims=True)) + 1e-05) * gain + bias

def gelu_value(upward):
    return 0.5 * upward * (1.0 + jax.scipy.special.erf(upward * math.sqrt(0.5)))

def rotate(heads, cosine, sine):
    half = ROT // 2
    first = heads[..., :half]
    second = heads[..., half:ROT]
    return jnp.concatenate([first * cosine - second * sine, second * cosine + first * sine, heads[..., ROT:]], -1)

def attend(query, keys, values, segment_ids):
    scores = jnp.einsum('gqhd,gkhd->ghqk', query, keys, precision=HIGHEST) * HEAD_DIM ** (-0.5)
    scores = low_back(scores)
    index = jnp.arange(SEQ)
    allowed = (segment_ids[:, None, :, None] == segment_ids[:, None, None, :]) & (index[:, None] >= index[None, :])
    scores = jnp.where(allowed, scores, -1000000000.0)
    top = lax.optimization_barrier(jnp.max(scores, -1, keepdims=True))
    total = top + jnp.log(lax.optimization_barrier(jnp.sum(jnp.exp(scores - top), -1, keepdims=True)))
    probs = low(jnp.exp(scores - total))
    return jnp.einsum('ghqk,gkhd->gqhd', probs, values, precision=HIGHEST)

def attend_group(packed):
    return jax.checkpoint(attend)(*packed)

def layer(hidden, weights, segment_ids, cosine, sine):
    attention_gain, attention_bias, joint_weight, joint_bias, output_weight, output_bias, feed_gain, feed_bias, up_weight, up_bias, down_weight, down_bias = weights
    lead = hidden.shape[:-1]
    normed = low(layer_norm(hidden, attention_gain, attention_bias))
    joint = low_back(jnp.dot(normed, joint_weight, precision=HIGHEST) + joint_bias)
    split = lead + (HEADS, HEAD_DIM)
    query = low(rotate(joint[..., :D].reshape(split), cosine, sine))
    keys = low(rotate(joint[..., D:2 * D].reshape(split), cosine, sine))
    values = low(joint[..., 2 * D:].reshape(split))
    group = math.gcd(MB * SEQS, max(1, 4096 // SEQ))

    def regroup(array):
        return array.reshape((-1, group) + array.shape[1:])
    context = lax.map(attend_group, (regroup(query), regroup(keys), regroup(values), regroup(segment_ids)))
    context = low(low_back(context.reshape(lead + (D,))))
    attended = jnp.dot(context, output_weight, precision=HIGHEST) + output_bias
    feed = low(layer_norm(hidden, feed_gain, feed_bias))
    upward = low_back(jnp.dot(feed, up_weight, precision=HIGHEST) + up_bias)
    active = low(gelu_value(upward))
    return hidden + attended + jnp.dot(active, down_weight, precision=HIGHEST) + down_bias

def reference(inputs, cotangent, segments, positions, attention_gain, attention_bias, joint_weight, joint_bias, output_weight, output_bias, feed_gain, feed_bias, up_weight, up_bias, down_weight, down_bias):
    params = tuple((array.astype(jnp.float32) for array in (attention_gain, attention_bias, joint_weight, joint_bias, output_weight, output_bias, feed_gain, feed_bias, up_weight, up_bias, down_weight, down_bias)))
    lead = (MB * SEQS, SEQ)
    segment_ids = segments.reshape(lead)
    half = ROT // 2
    rates = 10000.0 ** (-2.0 * jnp.arange(half, dtype=jnp.float32) / ROT)
    angle = positions.reshape(lead + (1, 1)).astype(jnp.float32) * rates
    cosine = jnp.cos(angle)
    sine = jnp.sin(angle)
    start = inputs.astype(jnp.float32).reshape(lead + (D,))

    def forward(shifts, weights):
        hidden = start
        results = []
        for section in range(SECTIONS):
            hidden = layer(hidden + shifts[section], tuple((item[section] for item in weights)), segment_ids, cosine, sine)
            if section + 1 < SECTIONS:
                hidden = low_back(low(hidden))
            results.append(hidden)
        return jnp.stack(results)
    shifts = jnp.zeros((SECTIONS,) + lead + (D,), jnp.float32)
    outputs, pull = jax.vjp(forward, shifts, params)
    upstream = jnp.zeros_like(outputs).at[SECTIONS - 1].set(cotangent.astype(jnp.float32).reshape(lead + (D,)))
    shift_grads, grads = pull(upstream)
    whole = (SECTIONS, MB, SEQS, SEQ, D)
    return (outputs.reshape(whole).astype(jnp.bfloat16), shift_grads.reshape(whole).astype(jnp.bfloat16), grads[0], grads[1], grads[2], grads[3], grads[4], grads[5], grads[6], grads[7], grads[8], grads[9], grads[10], grads[11])
```

```python
import functools
import math

import jax
import jax.numpy as jnp
from jax import lax
from jax.experimental import pallas as pl
from jax.experimental.pallas import tpu as pltpu
from jax.sharding import Mesh
from jax.sharding import PartitionSpec as P

D = 1024
HEAD_DIM = 64
ROT = 16
SEQ = 256
LOCAL = 256
FEED = 1024
HERE = LOCAL // HEAD_DIM
EPSILON = 1e-05
LOW = jnp.bfloat16
FULL = jnp.float32
VMEM = 56 * 1024 * 1024


def shift(block, axis, distance):
    size = lax.axis_size(axis)
    return lax.ppermute(block, axis, [(i, (i + distance) % size) for i in range(size)])


def gather_four(block, axis, dim):
    me = lax.axis_index(axis)
    whole = jnp.zeros(block.shape[:dim] + (4,) + block.shape[dim:], block.dtype)
    parts = [(0, block)] + [(d, shift(block, axis, d)) for d in (1, 3, 2)]
    for distance, part in parts:
        whole = lax.dynamic_update_slice_in_dim(
            whole, jnp.expand_dims(part, dim), (me - distance) % 4, dim
        )
    return whole


def scatter_four(block, axis, dim):
    me = lax.axis_index(axis)

    def quarter(index):
        return lax.dynamic_index_in_dim(block, index % 4, dim, False)

    total = quarter(me).astype(FULL)
    for distance in (1, 3, 2):
        total = total + shift(quarter(me + distance), axis, distance).astype(FULL)
    return total


def in_order(index, own, other, dim):
    return jnp.where(
        index == 0,
        jnp.concatenate([own, other], dim),
        jnp.concatenate([other, own], dim),
    )


def pair(block, axis, dim):
    return in_order(lax.axis_index(axis), block, shift(block, axis, 1), dim)


def dot(left, right):
    return jnp.dot(left, right, preferred_element_type=FULL)


def dot_back(left, right):
    return lax.dot_general(left, right, (((1,), (1,)), ((), ())), preferred_element_type=FULL)


def dot_over(left, right):
    return lax.dot_general(left, right, (((0,), (0,)), ((), ())), preferred_element_type=FULL)


def turn(heads, cosine, sine):
    lane = lax.broadcasted_iota(jnp.int32, heads.shape, 1) % HEAD_DIM
    partner = jnp.where(
        lane < ROT // 2,
        pltpu.roll(heads, LOCAL - ROT // 2, 1),
        pltpu.roll(heads, ROT // 2, 1),
    )
    return heads * cosine + partner * sine


def normalize(hidden):
    centred = hidden - jnp.mean(hidden, -1, keepdims=True)
    scale = lax.rsqrt(jnp.mean(centred * centred, -1, keepdims=True) + EPSILON)
    return centred * scale, scale


def head_lanes(head):
    lane = lax.broadcasted_iota(jnp.int32, (SEQ, LOCAL), 1)
    return lane // HEAD_DIM == head


def allowed_keys(seg_row, seg_col):
    query = lax.broadcasted_iota(jnp.int32, (SEQ, SEQ), 0)
    key = lax.broadcasted_iota(jnp.int32, (SEQ, SEQ), 1)
    return (seg_col == seg_row) & (query >= key)


def forward_kernel(
    keep, hidden, seg_row, seg_col, cosine, sine, params, w_query, w_pair, w_out, w_up, w_down, *out
):
    normed, _ = normalize(hidden[0].astype(FULL))
    first = (normed * params[0:1] + params[1:2]).astype(LOW)
    second = (normed * params[2:3] + params[3:4]).astype(LOW)
    cos = jnp.concatenate([cosine[0]] * 2, 1)
    sin = jnp.concatenate([sine[0]] * 2, 1)
    query = turn(dot(first, w_query[...]) + params[4:5, :LOCAL], cos, sin)
    both = dot(first, w_pair[...]) + params[4:5, LOCAL : 3 * LOCAL]
    keys = turn(both[:, :LOCAL], cos, sin).astype(LOW)
    values = both[:, LOCAL:].astype(LOW)
    allowed = allowed_keys(seg_row[0], seg_col[0])
    context = jnp.zeros((SEQ, LOCAL), FULL)
    lanes = lax.broadcasted_iota(jnp.int32, (SEQ, 128), 1)
    kept_lse = jnp.zeros((SEQ, 128), FULL)
    for head in range(HERE):
        mine = head_lanes(head)
        scores = dot_back(jnp.where(mine, query, 0.0).astype(LOW), keys) * HEAD_DIM**-0.5
        scores = jnp.where(allowed, scores, -1000000000.0)
        top = jnp.max(scores, -1, keepdims=True)
        weight = jnp.exp(scores - top)
        total = jnp.sum(weight, -1, keepdims=True)
        probs = (weight * (1.0 / total)).astype(LOW)
        context = jnp.where(mine, dot(probs, values), context)
        if keep:
            kept_lse = jnp.where(lanes == head, top + jnp.log(total), kept_lse)
    context = context.astype(LOW)
    upward = dot(second, w_up[...]) + params[5:6]
    half = 0.5 * (1.0 + lax.erf(upward * math.sqrt(0.5)))
    active = (upward * half).astype(LOW)
    out[0][0] = (dot(context, w_out[...]) + dot(active, w_down[...])).astype(LOW)
    if keep:
        slope = half + upward * jnp.exp(-0.5 * upward * upward) * math.sqrt(0.5 / math.pi)
        out[1][0] = first
        out[2][0] = second
        out[3][0] = query.astype(LOW)
        out[4][0] = keys
        out[5][0] = values
        out[6][0] = kept_lse
        out[7][0] = context
        out[8][0] = active
        out[9][0] = slope.astype(LOW)


def backward_kernel(
    keep,
    grad,
    hidden,
    seg_row,
    seg_col,
    cosine,
    sine,
    params,
    w_query,
    w_pair,
    w_out,
    w_up,
    w_down,
    query_in,
    keys_in,
    values_in,
    lse_in,
    slope,
    *out,
):
    g = grad[0]
    normed, scale = normalize(hidden[0].astype(FULL))
    up_grad = (dot_back(g, w_down[...]) * slope[0].astype(FULL)).astype(LOW)
    second_grad = dot_back(up_grad, w_up[...])
    context_grad = dot_back(g, w_out[...])
    context_low = context_grad.astype(LOW)
    query = query_in[0]
    keys = keys_in[0]
    values = values_in[0]
    query_full = query.astype(FULL)
    allowed = allowed_keys(seg_row[0], seg_col[0])
    query_grad = jnp.zeros((SEQ, LOCAL), FULL)
    keys_grad = jnp.zeros((SEQ, LOCAL), FULL)
    values_grad = jnp.zeros((SEQ, LOCAL), FULL)
    for head in range(HERE):
        mine = head_lanes(head)
        scores = dot_back(jnp.where(mine, query_full, 0.0).astype(LOW), keys) * HEAD_DIM**-0.5
        scores = jnp.where(allowed, scores, -1000000000.0)
        probs = jnp.exp(scores - lse_in[0][:, head : head + 1])
        probs_grad = dot_back(jnp.where(mine, context_grad, 0.0).astype(LOW), values)
        scores_grad = (
            probs * (probs_grad - jnp.sum(probs * probs_grad, -1, keepdims=True))
        ).astype(LOW)
        query_grad = jnp.where(mine, dot(scores_grad, keys), query_grad)
        keys_grad = jnp.where(mine, dot_over(scores_grad, query), keys_grad)
        values_grad = jnp.where(mine, dot_over(probs.astype(LOW), context_low), values_grad)
    cos = jnp.concatenate([cosine[0]] * 2, 1)
    sin = -jnp.concatenate([sine[0]] * 2, 1)
    query_low = turn(query_grad * HEAD_DIM**-0.5, cos, sin).astype(LOW)
    pair_low = jnp.concatenate(
        [turn(keys_grad * HEAD_DIM**-0.5, cos, sin), values_grad], 1
    ).astype(LOW)
    first_grad = dot_back(query_low, w_query[...]) + dot_back(pair_low, w_pair[...])
    inner = first_grad * params[0:1] + second_grad * params[2:3]
    out[0][0] = (
        scale
        * (
            inner
            - jnp.mean(inner, -1, keepdims=True)
            - normed * jnp.mean(inner * normed, -1, keepdims=True)
        )
    ).astype(LOW)
    if keep:
        out[1][0] = up_grad
        out[2][0] = query_low
        out[3][0] = pair_low
        out[4][0] = jnp.zeros((8, D), FULL)
        for row, item in enumerate(
            (
                first_grad * normed,
                first_grad,
                second_grad * normed,
                second_grad,
                up_grad.astype(FULL),
                g.astype(FULL),
                query_low.astype(FULL),
                pair_low.astype(FULL),
            )
        ):
            out[4][0, row : row + 1, : item.shape[1]] = jnp.sum(item, 0, keepdims=True)


def per_sequence(*shape):
    return pl.BlockSpec((1,) + shape, lambda i: (i,) + (0,) * len(shape))


def resident(*shape):
    return pl.BlockSpec(shape, lambda i: (0,) * len(shape))


LAYER_SPECS = [
    resident(8, D),
    resident(D, LOCAL),
    resident(D, 2 * LOCAL),
    resident(LOCAL, D),
    resident(D, FEED),
    resident(FEED, D),
]
PLACE_SPECS = [
    per_sequence(1, SEQ),
    per_sequence(SEQ, 1),
    per_sequence(SEQ, 128),
    per_sequence(SEQ, 128),
]
SAVED = (
    (D, LOW),
    (D, LOW),
    (LOCAL, LOW),
    (LOCAL, LOW),
    (LOCAL, LOW),
    (128, FULL),
    (LOCAL, LOW),
    (FEED, LOW),
    (FEED, LOW),
)


def forward(hidden, place, layer, keep):
    count = hidden.shape[0]
    widths = ((D, LOW),) + (SAVED if keep else ())
    return pl.pallas_call(
        functools.partial(forward_kernel, keep),
        grid=(count,),
        in_specs=[per_sequence(SEQ, D)] + PLACE_SPECS + LAYER_SPECS,
        out_specs=[per_sequence(SEQ, width) for width, _ in widths],
        out_shape=[jax.ShapeDtypeStruct((count, SEQ, width), kind) for width, kind in widths],
        compiler_params=pltpu.CompilerParams(vmem_limit_bytes=VMEM),
        cost_estimate=pl.CostEstimate(
            flops=count * SEQ * 6 * D * D, bytes_accessed=count * 4 * D * D, transcendentals=0
        ),
        name="layer_forward",
    )(hidden, *place, *layer)


def backward(grad, hidden, place, layer, saved, keep):
    count = hidden.shape[0]
    shapes = [((SEQ, D), LOW)]
    if keep:
        shapes += [
            ((SEQ, FEED), LOW),
            ((SEQ, LOCAL), LOW),
            ((SEQ, 2 * LOCAL), LOW),
            ((8, D), FULL),
        ]
    return pl.pallas_call(
        functools.partial(backward_kernel, keep),
        grid=(count,),
        in_specs=[per_sequence(SEQ, D)] * 2
        + PLACE_SPECS
        + LAYER_SPECS
        + [
            per_sequence(SEQ, LOCAL),
            per_sequence(SEQ, LOCAL),
            per_sequence(SEQ, LOCAL),
            per_sequence(SEQ, 128),
            per_sequence(SEQ, FEED),
        ],
        out_specs=[per_sequence(*shape) for shape, _ in shapes],
        out_shape=[jax.ShapeDtypeStruct((count,) + shape, kind) for shape, kind in shapes],
        compiler_params=pltpu.CompilerParams(vmem_limit_bytes=VMEM),
        cost_estimate=pl.CostEstimate(
            flops=count * SEQ * 6 * D * D, bytes_accessed=count * 4 * D * D, transcendentals=0
        ),
        name="layer_backward",
    )(grad, hidden, *place, *layer, saved[2], saved[3], saved[4], saved[5], saved[8])


SMALL = (32, 32, 96, 32, 32, 32, 128, 32)


def fetch_layer(small, joint_weight, output_weight, up_weight, down_weight):
    c = lax.axis_index("ctx")
    k = lax.axis_index("core")
    quarter = 2 * c + k
    joint_cut = joint_weight.reshape(32, 3, 4, 4, HEAD_DIM)
    joint_parts = [joint_cut[:, :, :, q].reshape(32, 3 * LOCAL) for q in range(4)]
    up_cut = up_weight.reshape(32, 16, 2, 2, HEAD_DIM)
    up_parts = [up_cut[:, :, q % 2, q // 2].reshape(32, FEED) for q in range(4)]

    def columns(index):
        return [lax.select_n(index, *joint_parts), lax.select_n(index, *up_parts)]

    flat = jnp.concatenate(small + (jnp.zeros((512 - sum(SMALL),), LOW),)).reshape(4, 128)
    flat = jnp.concatenate([flat, jnp.zeros((28, 128), LOW)], 0)
    shared = [output_weight, flat]
    own = jnp.concatenate(columns(quarter) + shared, 1)
    other = shift(jnp.concatenate(columns(quarter ^ 1) + shared, 1), "core", 1)
    block = in_order(k, own, other, 0)
    joint, up, out, flat = jnp.split(block, (768, 1792, 2816), 1)
    down = lax.dynamic_slice_in_dim(down_weight, c * 64, 64, 0)
    query = jnp.concatenate([joint[:, :LOCAL], flat], 1)
    mixed = gather_four(jnp.concatenate([out, query], 1), "x", 0)
    keyed = gather_four(joint[:, LOCAL:], "y", 0)
    out = lax.dynamic_index_in_dim(mixed, quarter, 0, False)[:, :D]
    out = gather_four(out, "y", 0).reshape(LOCAL, D)
    query = gather_four(mixed[:, :, D:], "y", 0).reshape(D, LOCAL + 128)
    keyed = gather_four(keyed, "x", 1).reshape(D, 2 * LOCAL)
    up = gather_four(up, "x", 0)
    down = gather_four(down, "y", 0)
    up = gather_four(up, "y", 0).reshape(D, FEED)
    down = gather_four(down, "x", 1).reshape(FEED, D)
    flat = query[:, LOCAL:].reshape(32, 32, 128)[:, :4].reshape(32, 512)
    edges = [sum(SMALL[:i]) for i in range(len(SMALL) + 1)]
    small = [flat[:, a:b].reshape(-1).astype(FULL) for a, b in zip(edges, edges[1:])]
    joint_bias = lax.dynamic_index_in_dim(
        small[2].reshape(3, 4, 4, HEAD_DIM), quarter, 2, False
    ).reshape(-1)
    up_bias = small[6].reshape(16, 2, 2, HEAD_DIM)
    up_bias = lax.dynamic_index_in_dim(
        lax.dynamic_index_in_dim(up_bias, c, 2, False), k, 1, False
    ).reshape(-1)
    params = jnp.stack(
        [
            small[0],
            small[1],
            small[4],
            small[5],
            jnp.pad(joint_bias, (0, D - 3 * LOCAL)),
            up_bias,
            small[3] + small[7],
            jnp.zeros((D,), FULL),
        ]
    )
    return params, query, keyed, out, up, down


def both_quarters(block):
    k = lax.axis_index("core")
    rows = block.astype(LOW).reshape(2, 32, -1)
    own = lax.dynamic_index_in_dim(rows, k, 0)
    other = shift(lax.dynamic_index_in_dim(rows, 1 - k, 0), "core", 1)
    return pair(in_order(k, own, other, 0), "ctx", 0)


def summed_quarters(block):
    k = lax.axis_index("core")
    rows = block.astype(LOW).reshape(2, 32, -1)
    other = shift(lax.dynamic_index_in_dim(rows, 1 - k, 0, False), "core", 1)
    total = (lax.dynamic_index_in_dim(rows, k, 0, False).astype(FULL) + other.astype(FULL)).astype(
        LOW
    )
    return total.astype(FULL) + shift(total, "ctx", 1).astype(FULL)


def chunks(block):
    return block.astype(LOW).reshape(4, 4, 64, -1)


def return_down(term):
    block = scatter_four(chunks(term), "x", 1).astype(LOW)
    block = scatter_four(block, "y", 0).astype(LOW)
    return pair(block, "ctx", 0).astype(FULL)


def return_up(term):
    block = scatter_four(chunks(term), "y", 0).astype(LOW)
    block = both_quarters(scatter_four(block, "x", 0))
    return block.reshape(2, 2, 32, 16, HEAD_DIM).transpose(2, 3, 1, 0, 4).reshape(32, -1).astype(FULL)


def return_out(term):
    quarter = 2 * lax.axis_index("ctx") + lax.axis_index("core")
    block = scatter_four(term.astype(LOW).reshape(4, 64, D), "y", 0).astype(LOW)
    block = jnp.where(jnp.arange(4)[:, None, None] == quarter, block[None], jnp.zeros_like(block[None]))
    return summed_quarters(scatter_four(block, "x", 0))


def return_joint(query_term, pair_term, small_terms):
    block = jnp.concatenate([query_term.astype(LOW), small_terms.astype(LOW)], 1)
    block = scatter_four(chunks(block), "y", 0).astype(LOW)
    other = scatter_four(chunks(pair_term), "x", 1).astype(LOW)
    block = scatter_four(block, "x", 0)
    other = scatter_four(other, "y", 0)
    joint = both_quarters(jnp.concatenate([block[:, :LOCAL], other], 1))
    joint = joint.reshape(4, 32, 3, 4, HEAD_DIM).transpose(1, 2, 3, 0, 4).reshape(32, -1)
    flat = summed_quarters(block[:, LOCAL:])[:4].reshape(-1)
    edges = [sum(SMALL[:i]) for i in range(len(SMALL) + 1)]
    return joint.astype(FULL), [flat[a:b] for a, b in zip(edges, edges[1:])]


def pack_small(sums):
    c = lax.axis_index("ctx")
    k = lax.axis_index("core")
    quarter = 2 * c + k
    joint = jnp.concatenate([sums[6, :LOCAL], sums[7, : 2 * LOCAL]]).reshape(3, 4, 1, HEAD_DIM)
    joint = jnp.where(jnp.arange(4)[:, None] == quarter, joint, 0.0)
    where_up = (jnp.arange(2)[:, None, None] == k) & (jnp.arange(2)[:, None] == c)
    up = jnp.where(where_up, sums[4].reshape(16, 1, 1, HEAD_DIM), 0.0)
    grads = sums[5] * 0.25
    items = (sums[0], sums[1], joint, grads, sums[2], sums[3], up, grads)
    flat = [item.reshape(32, -1) for item in items] + [jnp.zeros((32, 512 - sum(SMALL)), FULL)]
    flat = jnp.concatenate(flat, 1).reshape(32, 4, 128)
    return jnp.pad(flat, ((0, 0), (0, 28), (0, 0))).reshape(D, 128)


def reduce_own(partial):
    c = lax.axis_index("ctx")
    k = lax.axis_index("core")
    other = shift(lax.dynamic_index_in_dim(partial, 1 - k, 0, False), "core", 1)
    total = lax.dynamic_index_in_dim(partial, k, 0, False).astype(FULL) + other.astype(FULL)
    half = total.reshape(2, SEQ // 2, D)
    other = shift(lax.dynamic_index_in_dim(half, 1 - c, 0, False).astype(LOW), "ctx", 1)
    return lax.dynamic_index_in_dim(half, c, 0, False) + other.astype(FULL)


def hand_on(block, start, end):
    c = lax.axis_index("ctx")
    same = lax.ppermute(
        block, ("section", "ctx"), [(2 * start, 2 * end), (2 * start + 1, 2 * end + 1)]
    )
    flip = lax.ppermute(
        block, ("section", "ctx"), [(2 * start, 2 * end + 1), (2 * start + 1, 2 * end)]
    )
    whole = in_order(c, same, flip, 0)
    return pair(whole[None], "core", 0)


def shards(
    inputs,
    cotangent,
    segments,
    positions,
    attention_gain,
    attention_bias,
    joint_weight,
    joint_bias,
    output_weight,
    output_bias,
    feed_gain,
    feed_bias,
    up_weight,
    up_bias,
    down_weight,
    down_bias,
):
    section = lax.axis_index("section")
    count = inputs.shape[0]
    layer = fetch_layer(
        (
            attention_gain[0],
            attention_bias[0],
            joint_bias[0],
            output_bias[0],
            feed_gain[0],
            feed_bias[0],
            up_bias[0],
            down_bias[0],
        ),
        joint_weight[0],
        output_weight[0],
        up_weight[0],
        down_weight[0],
    )
    bias = layer[0][6]
    whole_in = pair(pair(inputs, "ctx", 2), "core", 1)
    whole_grad = pair(pair(cotangent, "ctx", 2), "core", 1)
    seg = pair(segments, "core", 1)
    pos = pair(pair(positions, "ctx", 2), "core", 1)
    lane = jnp.arange(128) % HEAD_DIM
    rates = jnp.where(lane < ROT, 10000.0 ** (-2.0 * (lane % (ROT // 2)).astype(FULL) / ROT), 0.0)
    angle = pos.astype(FULL)[..., None] * rates
    cosine = jnp.cos(angle)
    sine = jnp.sin(angle) * jnp.where(lane < ROT // 2, -1.0, 1.0)
    places = [(seg[m][:, None, :], seg[m][:, :, None], cosine[m], sine[m]) for m in range(count)]
    own_in = inputs[:, 0].astype(FULL)
    hidden = []
    for m in range(count):
        (partial,) = forward(whole_in[m], places[m], layer, False)
        result = (own_in[m] + bias + reduce_own(partial)).astype(LOW)
        hidden.append(jnp.where(section == 0, whole_in[m], hand_on(result, 0, 1)))
    c = lax.axis_index("ctx")
    k = lax.axis_index("core")
    saved = []
    outputs = []
    for m in range(count):
        partial, *kept = forward(hidden[m], places[m], layer, True)
        own = lax.dynamic_index_in_dim(hidden[m], k, 0, False).reshape(2, SEQ // 2, D)
        own = lax.dynamic_index_in_dim(own, c, 0, False).astype(FULL)
        outputs.append((own + bias + reduce_own(partial)).astype(LOW))
        saved.append(kept)
    own_grad = cotangent[:, 0].astype(FULL)
    grads = []
    for m in range(count):
        (partial,) = backward(whole_grad[m], hidden[m], places[m], layer, saved[m], False)
        result = (own_grad[m] + reduce_own(partial)).astype(LOW)
        grads.append(jnp.where(section == 1, whole_grad[m], hand_on(result, 1, 0)))
    grad_all = jnp.concatenate(grads, 0).reshape(-1, D)

    def all_tokens(index):
        return jnp.concatenate([kept[index] for kept in saved], 0).reshape(count * 2 * SEQ, -1)

    down_grad = return_down(dot_over(all_tokens(7), grad_all))
    out_grad = return_out(dot_over(all_tokens(6), grad_all))
    input_grads = []
    terms = []
    for m in range(count):
        partial, *more = backward(grads[m], hidden[m], places[m], layer, saved[m], True)
        own = lax.dynamic_index_in_dim(grads[m], k, 0, False).reshape(2, SEQ // 2, D)
        own = lax.dynamic_index_in_dim(own, c, 0, False).astype(FULL)
        input_grads.append((own + reduce_own(partial)).astype(LOW))
        terms.append(more)

    def all_terms(index):
        return jnp.concatenate([more[index] for more in terms], 0).reshape(count * 2 * SEQ, -1)

    up_grad = return_up(dot_over(all_tokens(1), all_terms(0)))
    sums = sum(jnp.sum(more[3], 0) for more in terms)
    first = all_tokens(0)
    joint_grad, small = return_joint(
        dot_over(first, all_terms(1)), dot_over(first, all_terms(2)), pack_small(sums)
    )
    section_out = jnp.stack(outputs)[None, :, None]
    input_grad = jnp.stack(input_grads)[None, :, None]
    return (
        section_out,
        input_grad,
        small[0][None],
        small[1][None],
        joint_grad[None],
        small[2][None],
        out_grad[None],
        small[3][None],
        small[4][None],
        small[5][None],
        up_grad[None],
        small[6][None],
        down_grad[None],
        small[7][None],
    )


def solution(mesh):
    finer = Mesh(mesh.devices.reshape(2, 2, 4, 4, 2), ("section", "ctx", "y", "x", "core"))
    fsdp = ("y", "x", "core")
    vector = P("section", fsdp)
    matrix = P("section", fsdp, None)
    tokens = P(None, fsdp, "ctx", None)
    kept = P("section", None, fsdp, "ctx", None)
    params = (
        vector,
        vector,
        matrix,
        vector,
        matrix,
        vector,
        vector,
        vector,
        matrix,
        vector,
        matrix,
        vector,
    )
    return jax.shard_map(
        shards,
        mesh=finer,
        in_specs=(tokens, tokens, P(None, fsdp, None), P(None, fsdp, "ctx")) + params,
        out_specs=(kept, kept) + params,
        check_vma=False,
    )
```

```python
import functools
import math

import jax
import jax.numpy as jnp
from jax import lax
from jax.experimental import pallas as pl
from jax.experimental.pallas import tpu as pltpu
from jax.sharding import Mesh
from jax.sharding import PartitionSpec as P

D = 1024
HEAD_DIM = 64
ROT = 16
SEQ = 256
LOCAL = 256
FEED = 1024
HERE = LOCAL // HEAD_DIM
EPSILON = 1e-05
LOW = jnp.bfloat16
FULL = jnp.float32
VMEM = 20 * 1024 * 1024


def shift(block, axis, distance):
    size = lax.axis_size(axis)
    return lax.ppermute(block, axis, [(i, (i + distance) % size) for i in range(size)])


def gather_rings(routes, first=(), second=()):
    *near, first = together(
        *[[shift(block, axis, 1), shift(block, axis, -1)] for block, axis, _ in routes],
        [shift(block, axis, 1) for block, axis in first],
    )
    cuts = [block.shape[-1] // 256 * 128 for block, _, _ in routes]
    *far, second = together(
        *[
            [shift(behind[..., :cut], axis, 1), shift(ahead[..., cut:], axis, -1)]
            for (_, axis, _), (behind, ahead), cut in zip(routes, near, cuts)
        ],
        [shift(item(*first), axis, 1) for item, axis in second],
    )
    result = []
    for (block, axis, dim), (behind, ahead), halves in zip(routes, near, far):
        me = lax.axis_index(axis)
        whole = jnp.zeros(block.shape[:dim] + (4,) + block.shape[dim:], block.dtype)
        opposite = jnp.concatenate(halves, -1)
        for distance, part in enumerate((block, behind, opposite, ahead)):
            whole = lax.dynamic_update_slice_in_dim(
                whole, jnp.expand_dims(part, dim), (me - distance) % 4, dim
            )
        result.append(whole)
    return result, first, second


def shift_pair(block, axis, apart):
    size = lax.axis_size(axis)
    return lax.ppermute(block, axis, [(i, i ^ apart) for i in range(size)])


def quarter_of(block, dim, index):
    return lax.dynamic_index_in_dim(block, index % 4, dim, False)


def ring_start(block, axis, dim):
    far = quarter_of(block, dim, lax.axis_index(axis) + 2)
    cut = far.shape[-1] // 2
    return [shift(far[..., :cut], axis, 1), shift(far[..., cut:], axis, -1)]


def ring_next(block, axis, dim, up, down):
    me = lax.axis_index(axis)
    cut = up.shape[-1]
    ahead = quarter_of(block, dim, me + 1)
    behind = quarter_of(block, dim, me - 1)
    ahead = jnp.concatenate([plus(ahead[..., :cut], up), ahead[..., cut:]], -1)
    behind = jnp.concatenate([behind[..., :cut], plus(behind[..., cut:], down)], -1)
    return [shift(ahead, axis, 1), shift(behind, axis, -1)]


def direct(block, axis, dim):
    me = lax.axis_index(axis)
    return [shift(quarter_of(block, dim, me + d), axis, d) for d in (1, 3, 2)]


def together(*groups):
    flat = lax.optimization_barrier(tuple(item for group in groups for item in group))
    result = []
    for group in groups:
        result.append(flat[: len(group)])
        flat = flat[len(group) :]
    return result


def plus(*terms):
    return sum(term.astype(FULL) for term in terms).astype(LOW)


def after(block, *others):
    return lax.optimization_barrier((block,) + others)[0]


def in_order(index, own, other, dim):
    return jnp.where(
        index == 0,
        jnp.concatenate([own, other], dim),
        jnp.concatenate([other, own], dim),
    )


def pair(block, axis, dim):
    return in_order(lax.axis_index(axis), block, shift(block, axis, 1), dim)


def dot(left, right):
    return jnp.dot(left, right, preferred_element_type=FULL)


def dot_back(left, right):
    return lax.dot_general(left, right, (((1,), (1,)), ((), ())), preferred_element_type=FULL)


def dot_over(left, right):
    return lax.dot_general(left, right, (((0,), (0,)), ((), ())), preferred_element_type=FULL)


def turn(heads, cosine, sine):
    lane = lax.broadcasted_iota(jnp.int32, heads.shape, 1) % HEAD_DIM
    partner = jnp.where(
        lane < ROT // 2,
        pltpu.roll(heads, LOCAL - ROT // 2, 1),
        pltpu.roll(heads, ROT // 2, 1),
    )
    return heads * cosine + partner * sine


def normalize(hidden):
    centred = hidden - jnp.mean(hidden, -1, keepdims=True)
    scale = lax.rsqrt(jnp.mean(centred * centred, -1, keepdims=True) + EPSILON)
    return centred * scale, scale


def head_lanes(head):
    lane = lax.broadcasted_iota(jnp.int32, (SEQ, LOCAL), 1)
    return lane // HEAD_DIM == head


def head_stack(block):
    full = block.astype(FULL)
    copies = [jnp.where(head_lanes(head), full, 0.0) for head in range(HERE)]
    return jnp.concatenate(copies, 0).astype(LOW)


def head_pick(block):
    result = block[0]
    for head in range(1, HERE):
        result = jnp.where(head_lanes(head), block[head], result)
    return result


def by_head(block):
    return block.reshape(HERE, SEQ, SEQ)


def allowed_keys(seg_row, seg_col):
    query = lax.broadcasted_iota(jnp.int32, (SEQ, SEQ), 0)
    key = lax.broadcasted_iota(jnp.int32, (SEQ, SEQ), 1)
    return (seg_col == seg_row) & (query >= key)


def flat(ref):
    return ref[...].reshape(ref.shape[0] * ref.shape[1], ref.shape[2])


def rows(seq):
    return pl.ds(seq * SEQ, SEQ)


def forward_kernel(
    keep, hidden, seg_row, seg_col, cosine, sine, params, weights, w_out, w_down, partial, *out
):
    normed, _ = normalize(flat(hidden).astype(FULL))
    first = (normed * params[0:1] + params[1:2]).astype(LOW)
    second = (normed * params[2:3] + params[3:4]).astype(LOW)
    cos = jnp.concatenate([flat(cosine)] * 2, 1)
    sin = jnp.concatenate([flat(sine)] * 2, 1)
    joint = dot(first, weights[:, JOINT]) + params[4:5, : 3 * LOCAL]
    query = turn(joint[:, :LOCAL], cos, sin)
    keys = turn(joint[:, LOCAL : 2 * LOCAL], cos, sin).astype(LOW)
    values = joint[:, 2 * LOCAL :].astype(LOW)
    contexts = []
    for seq in range(hidden.shape[0]):
        part = slice(seq * SEQ, seq * SEQ + SEQ)
        scores = by_head(dot_back(head_stack(query[part]), keys[part]))
        scores = jnp.where(
            allowed_keys(seg_row[seq], seg_col[seq])[None],
            scores * HEAD_DIM**-0.5,
            -1000000000.0,
        )
        top = jnp.max(scores, -1, keepdims=True)
        weight = jnp.exp(scores - top)
        total = jnp.sum(weight, -1, keepdims=True)
        probs = (weight * (1.0 / total)).astype(LOW).reshape(HERE * SEQ, SEQ)
        contexts.append(head_pick(by_head(dot(probs, values[part]))).astype(LOW))
        if keep:
            out[5][pl.ds(seq * HERE, HERE)] = top + jnp.log(total)
    context = jnp.concatenate(contexts, 0)
    upward = dot(second, weights[:, UP]) + params[5:6]
    half = 0.5 * (1.0 + lax.erf(upward * math.sqrt(0.5)))
    active = (upward * half).astype(LOW)
    result = dot(context, w_out[:, :D]) + dot(active, w_down[...])
    if keep:
        out[7][...] = active
        slope = half + upward * jnp.exp(-0.5 * upward * upward) * math.sqrt(0.5 / math.pi)
        out[8][...] = slope.astype(LOW)
    partial[...] = result.astype(LOW).reshape(partial.shape)
    if keep:
        out[0][...] = first
        out[1][...] = second
        out[2][...] = query.astype(LOW)
        out[3][...] = keys
        out[4][...] = values
        out[6][...] = context


def backward_kernel(
    keep,
    grad,
    hidden,
    seg_row,
    seg_col,
    cosine,
    sine,
    params,
    weights,
    w_out,
    w_down,
    query_in,
    keys_in,
    values_in,
    lse_in,
    slope,
    partial,
    *out,
):
    g = flat(grad)
    context_grad = dot_back(g, w_out[:, :D])
    turned = []
    for seq in range(hidden.shape[0]):
        part = slice(seq * SEQ, seq * SEQ + SEQ)
        query = query_in[rows(seq)]
        keys = keys_in[rows(seq)]
        values = values_in[rows(seq)]
        queries = head_stack(query)
        contexts = head_stack(context_grad[part])
        scores = by_head(dot_back(queries, keys))
        scores = jnp.where(
            allowed_keys(seg_row[seq], seg_col[seq])[None],
            scores * HEAD_DIM**-0.5,
            -1000000000.0,
        )
        probs = jnp.exp(scores - lse_in[pl.ds(seq * HERE, HERE)])
        probs_grad = by_head(dot_back(contexts, values))
        scores_grad = probs * (probs_grad - jnp.sum(probs * probs_grad, -1, keepdims=True))
        scores_grad = scores_grad.astype(LOW).reshape(HERE * SEQ, SEQ)
        probs = probs.astype(LOW).reshape(HERE * SEQ, SEQ)
        query_grad = head_pick(by_head(dot(scores_grad, keys)))
        keys_grad = dot_over(scores_grad, queries)
        values_grad = dot_over(probs, contexts)
        cos = jnp.concatenate([cosine[seq]] * 2, 1)
        sin = -jnp.concatenate([sine[seq]] * 2, 1)
        turned.append(
            jnp.concatenate(
                [
                    turn(query_grad * HEAD_DIM**-0.5, cos, sin),
                    turn(keys_grad * HEAD_DIM**-0.5, cos, sin),
                    values_grad,
                ],
                1,
            ).astype(LOW)
        )
    joint_grad = jnp.concatenate(turned, 0)
    first_grad = dot_back(joint_grad, weights[:, JOINT])
    up_grad = (dot_back(g, w_down[...]) * slope[...].astype(FULL)).astype(LOW)
    second_grad = dot_back(up_grad, weights[:, UP])
    normed, scale = normalize(flat(hidden).astype(FULL))
    inner = first_grad * params[0:1] + second_grad * params[2:3]
    back = scale * (
        inner
        - jnp.mean(inner, -1, keepdims=True)
        - normed * jnp.mean(inner * normed, -1, keepdims=True)
    )
    partial[...] = back.astype(LOW).reshape(partial.shape)
    if keep:
        out[0][...] = up_grad
        out[1][...] = joint_grad
        out[2][...] = jnp.zeros(out[2].shape, FULL)
        for row, item in (
            (0, first_grad * normed),
            (1, first_grad),
            (2, second_grad * normed),
            (3, second_grad),
            (4, up_grad.astype(FULL)),
            (5, g.astype(FULL)),
            (6, joint_grad.astype(FULL)),
        ):
            out[2][row : row + 1, : item.shape[1]] = jnp.sum(item, 0, keepdims=True)


JOINT = slice(0, 3 * LOCAL)
UP = slice(3 * LOCAL, 3 * LOCAL + FEED)
SAVED = (
    (D, LOW),
    (D, LOW),
    (LOCAL, LOW),
    (LOCAL, LOW),
    (LOCAL, LOW),
    None,
    (LOCAL, LOW),
    (FEED, LOW),
    (FEED, LOW),
)


def call(kernel, name, operands, shapes):
    return pl.pallas_call(
        kernel,
        in_specs=[pl.BlockSpec(memory_space=pltpu.VMEM)] * len(operands),
        out_specs=[pl.BlockSpec(memory_space=pltpu.VMEM)] * len(shapes),
        out_shape=[jax.ShapeDtypeStruct(shape, kind) for shape, kind in shapes],
        compiler_params=pltpu.CompilerParams(vmem_limit_bytes=VMEM),
        cost_estimate=pl.CostEstimate(
            flops=2 * SEQ * 18 * D * D, bytes_accessed=8 * D * D, transcendentals=0
        ),
        name=name,
    )(*operands)


def forward(hidden, place, layer, keep):
    tokens = hidden.shape[0] * SEQ
    shapes = [(hidden.shape, LOW)]
    if keep:
        lse = ((hidden.shape[0] * HERE, SEQ, 1), FULL)
        shapes += [((tokens, item[0]), item[1]) if item else lse for item in SAVED]
    kernel = functools.partial(forward_kernel, keep)
    return call(kernel, "layer_forward", (hidden, *place, *layer), shapes)


def backward(grad, hidden, place, layer, saved, keep):
    tokens = hidden.shape[0] * SEQ
    shapes = [(hidden.shape, LOW)]
    if keep:
        shapes += [((tokens, FEED), LOW), ((tokens, 3 * LOCAL), LOW), ((8, D), FULL)]
    kernel = functools.partial(backward_kernel, keep)
    operands = (grad, hidden, *place, *layer, *saved[2:6], saved[8])
    return call(kernel, "layer_backward", operands, shapes)


def lower_upper(lower, upper, half):
    lane = lax.broadcasted_iota(jnp.int32, lower.shape, 1)
    if half == 0:
        return jnp.where(lane < HEAD_DIM, lower, pltpu.roll(upper, HEAD_DIM, 1))
    return jnp.where(lane < HEAD_DIM, pltpu.roll(lower, HEAD_DIM, 1), upper)


def choose_kernel(place, joint, up, out):
    c, k = place[0], place[1]

    def group(ref, index):
        return ref[:, pl.ds(pl.multiple_of(index * 128, 128), 128)].astype(FULL)

    for pair_ in range(6):
        lower = group(joint, 4 * pair_ + c)
        upper = group(joint, 4 * pair_ + 2 + c)
        here = slice(pair_ * 128, pair_ * 128 + 128)
        out[k, :, here] = lower_upper(lower, upper, 0).astype(LOW)
        out[1 - k, :, here] = lower_upper(lower, upper, 1).astype(LOW)
    for pair_ in range(8):
        here = slice(3 * LOCAL + pair_ * 128, 3 * LOCAL + pair_ * 128 + 128)
        for slot, core in ((0, k), (1, 1 - k)):
            lower = group(up, 4 * pair_ + core)
            upper = group(up, 4 * pair_ + 2 + core)
            block = jnp.where(
                jnp.zeros(lower.shape, jnp.int32) + c == 0,
                lower_upper(lower, upper, 0),
                lower_upper(lower, upper, 1),
            )
            out[slot, :, here] = block.astype(LOW)


def finish_kernel(
    place, block, down_in, out_own, out_other, sums, joint, out, up, down, *rest
):
    vectors, (whole, up_all, joint_all) = rest[:8], rest[8:]

    def quarter(c, k, column):
        return block[c, 32 * k : 32 * k + 32, column : column + 128].astype(FULL)

    def vector(c, k, column):
        return sums[2 * c + k, :, column : column + 128]

    for p in range(16):
        at = p // 2 * 128
        for k in range(2):
            here = slice((2 * p + k) * 128, (2 * p + k) * 128 + 128)
            up[0, :, here] = lower_upper(quarter(0, k, at), quarter(1, k, at), p % 2)
            up_all[:, here] = lower_upper(vector(0, k, at), vector(1, k, at), p % 2)
    for t in range(12):
        at = t // 2 * 128
        for c in range(2):
            here = slice((2 * t + c) * 128, (2 * t + c) * 128 + 128)
            joint[0, :, here] = lower_upper(
                quarter(c, 0, FEED + at), quarter(c, 1, FEED + at), t % 2
            )
            joint_all[:, here] = lower_upper(vector(c, 0, at), vector(c, 1, at), t % 2)
    joint_all[:, 3 * D :] = jnp.zeros((8, 128), FULL)
    for c in range(2):
        down[0, 64 * c : 64 * c + 64] = down_in[c].astype(FULL)
    out[0] = out_own[...].astype(FULL) + out_other[...].astype(FULL)
    whole[...] = sums[0] + sums[1] + sums[2] + sums[3]
    whole[5:6] = sums[0, 5:6]
    f = place[0]

    def lanes(ref, start, width):
        first = pl.multiple_of(start // 128 * 128, 128)
        return pltpu.roll(ref[:, pl.ds(first, width)], (width - start % 128) % width, 1)

    shares = lanes(whole, f * 32, 128)
    for index, row in ((0, 0), (1, 1), (3, 5), (4, 2), (5, 3), (7, 5)):
        vectors[index][...] = shares[row : row + 1, :32]
    vectors[2][...] = lanes(joint_all, f * 96, 256)[6:7, :96]
    vectors[6][...] = up_all[4:5, pl.ds(pl.multiple_of(f * 128, 128), 128)]


def term(left, right):
    return sum(dot_over(a[...], b[...]) for a, b in zip(left, right)).astype(LOW)


def down_kernel(*refs):
    active, grad = zip(refs[:2], refs[2:4])
    refs[4][...] = term(active, grad)


def weights_kernel(*refs):
    first, second, context, grad, joint_grad, up_grad = zip(refs[:6], refs[6:12])
    one, two = refs[12:]
    up = term(second, up_grad)
    one[:, :SPLIT] = up[:, :SPLIT]
    two[:, : FEED - SPLIT] = up[:, SPLIT:]
    out = term(context, grad)
    for y in range(4):
        for x in range(4):
            rows = slice((4 * y + x) * 64, (4 * y + x) * 64 + 64)
            one[rows, SPLIT:] = out[64 * y : 64 * y + 64, LOCAL * x : LOCAL * x + LOCAL]
    two[:, FEED - SPLIT :] = term(first, joint_grad)


SPLIT = 768


def simple_call(kernel, name, operands, shapes, scalars=0, scratch=()):
    return pl.pallas_call(
        kernel,
        in_specs=[pl.BlockSpec(memory_space=pltpu.SMEM)] * scalars
        + [pl.BlockSpec(memory_space=pltpu.VMEM)] * (len(operands) - scalars),
        out_specs=[pl.BlockSpec(memory_space=pltpu.VMEM)] * len(shapes),
        out_shape=[jax.ShapeDtypeStruct(shape, kind) for shape, kind in shapes],
        scratch_shapes=[pltpu.VMEM(shape, FULL) for shape in scratch],
        compiler_params=pltpu.CompilerParams(vmem_limit_bytes=VMEM),
        name=name,
    )(*operands)


SMALL = (32, 32, 96, 32, 32, 32, 128, 32)
EDGES = [sum(SMALL[:i]) for i in range(len(SMALL) + 1)]


def choose_columns(joint_weight, up_weight):
    c = lax.axis_index("ctx")
    k = lax.axis_index("core")
    (chosen,) = simple_call(
        choose_kernel,
        "choose_columns",
        (jnp.stack([c, k]), joint_weight, up_weight),
        [((2, 32, 3 * LOCAL + FEED), LOW)],
        1,
    )
    return in_order(k, chosen[0], shift(chosen[1], "core", 1), 0)


def fetch_layer(block, tokens, small, output_weight, down_weight):
    c = lax.axis_index("ctx")
    k = lax.axis_index("core")
    quarter = 2 * c + k
    weights = lax.all_gather(block, ("y", "x"), axis=0, tiled=True)
    vectors = jnp.concatenate(small + (jnp.zeros((512 - sum(SMALL),), LOW),)).reshape(4, 128)
    vectors = jnp.concatenate([vectors, jnp.zeros((28, 128), LOW)], 0)
    mixed = pair(after(jnp.concatenate([output_weight, vectors], 1), block), "core", 0)
    down = lax.dynamic_slice_in_dim(down_weight, c * 64, 64, 0)

    def sequence(own):
        return lambda other: in_order(c, own, other, 2)

    (mixed, down), first, second = gather_rings(
        [(mixed, "x", 0), (down, "y", 0)],
        [(tokens[0], "ctx")],
        [(sequence(tokens[0]), "core")],
    )
    inputs = in_order(k, sequence(tokens[0])(*first), *second, 1)
    out = lax.dynamic_index_in_dim(mixed, quarter, 0, False)[:, :D]
    vectors = mixed[:, :, D:].reshape(4, 2, 32, 128)[:, :, :8].reshape(64, 128)
    (out, down), first, second = gather_rings(
        [(jnp.concatenate([out, vectors], 1), "y", 0), (down, "x", 1)],
        [(tokens[1], "ctx")],
        [(sequence(tokens[1]), "core")],
    )
    cotangent = in_order(k, sequence(tokens[1])(*first), *second, 1)
    vectors = out[:, :, D:].reshape(32, 8, 128)[:, :4].reshape(32, 512)
    small = [vectors[:, a:b].reshape(-1).astype(FULL) for a, b in zip(EDGES, EDGES[1:])]
    joint_bias = lax.dynamic_index_in_dim(
        small[2].reshape(3, 4, 4, HEAD_DIM), quarter, 2, False
    ).reshape(-1)
    up_bias = small[6].reshape(16, 2, 2, HEAD_DIM)
    up_bias = lax.dynamic_index_in_dim(
        lax.dynamic_index_in_dim(up_bias, c, 2, False), k, 1, False
    ).reshape(-1)
    params = jnp.stack(
        [
            small[0],
            small[1],
            small[4],
            small[5],
            jnp.pad(joint_bias, (0, D - 3 * LOCAL)),
            up_bias,
            small[3] + small[7],
            jnp.zeros((D,), FULL),
        ]
    )
    layer = (params, weights, out.reshape(LOCAL, D + 128), down.reshape(FEED, D))
    return layer, inputs, cotangent


def return_layer(one, two, down, sums, beside, late):
    c = lax.axis_index("ctx")
    k = lax.axis_index("core")
    x = lax.axis_index("x")
    y = lax.axis_index("y")
    one = one.reshape(4, 4, 64, -1)
    two = two.reshape(4, 4, 64, -1)
    sums = sums + shift_pair(sums, "y", 1)
    ones, twos, (more, beside, core) = together(
        ring_start(one, "y", 0),
        ring_start(two, "x", 1),
        [shift_pair(sums, "y", 2), beside, late[1]],
    )
    sums = sums + more
    own, give = halves_of(late[0], core)
    ones, twos, (more, got) = together(
        ring_next(one, "y", 0, *ones),
        ring_next(two, "x", 1, *twos),
        [shift_pair(sums, "x", 1), shift(give, "ctx", 1)],
    )
    sums = sums + more
    one = plus(quarter_of(one, 0, y), *ones)
    two = plus(quarter_of(two, 1, x), *twos)
    out = one[:, :, SPLIT :].transpose(1, 0, 2).reshape(1, 64, D)
    out = jnp.where(
        jnp.arange(4)[:, None, None] == 2 * c + k, out, jnp.zeros_like(out)
    )
    one = jnp.concatenate([one[:, :, : SPLIT], out], -1)
    ones, twos, (more, down_more) = together(
        direct(one, "x", 0),
        direct(two, "y", 0),
        [shift_pair(sums, "x", 2), shift(down, "ctx", 1)],
    )
    sums = sums + more
    one = plus(quarter_of(one, 0, x), *ones)
    two = plus(quarter_of(two, 0, y), *twos)
    both = jnp.concatenate([one[:, :SPLIT], two, one[:, SPLIT:]], 1)
    both = both.reshape(2, 32, -1)
    width = FEED + 3 * LOCAL
    mine = take(both, k, 0)
    (other,), (more,) = together(
        [shift(take(both, 1 - k, 0), "core", 1)], [shift(sums, "core", 1)]
    )
    sums = in_order(k, sums[None], more[None], 0)
    block = in_order(k, mine[:, :width], other[:, :width], 0)
    out = plus(mine[:, width:], other[:, width:])
    (block_more, out_more, sums_more), _ = together(
        [shift(block, "ctx", 1), shift(out, "ctx", 1), shift(sums, "ctx", 1)], [beside]
    )
    place = (4 * y + x) * 2 + k
    vectors = [((1, width), FULL) for width in SMALL]
    joint, out, up, down, *vectors = simple_call(
        finish_kernel,
        "finish",
        (
            place[None],
            in_order(c, block[None], block_more[None], 0),
            in_order(c, down[None], down_more[None], 0),
            out,
            out_more,
            in_order(c, sums, sums_more, 0),
        ),
        [((1, 32, 3 * D), FULL), ((1, 32, D), FULL), ((1, 32, 4 * D), FULL), ((1, 128, D), FULL)]
        + vectors,
        1,
        ((8, D), (8, 4 * D), (8, 3 * D + 128)),
    )
    return joint, out, up, down, vectors, beside, own + got.astype(FULL)


def plus_full(left, right):
    return left.astype(FULL) + right.astype(FULL)


def take(block, index, dim):
    return lax.dynamic_index_in_dim(block, index, dim, False)


def over_cores(partial):
    k = lax.axis_index("core")
    return take(partial, k, 1), shift(take(partial, 1 - k, 1), "core", 1)


def halves_of(mine, other):
    c = lax.axis_index("ctx")
    total = plus_full(mine, other).reshape(-1, 2, SEQ // 2, D)
    return take(total, c, 1), take(total, 1 - c, 1).astype(LOW)


def sum_cores(partial):
    return halves_of(*over_cores(partial))


def send_on(block, start, end):
    same = lax.ppermute(
        block, ("section", "ctx"), [(2 * start, 2 * end), (2 * start + 1, 2 * end + 1)]
    )
    flip = lax.ppermute(
        block, ("section", "ctx"), [(2 * start, 2 * end + 1), (2 * start + 1, 2 * end)]
    )
    return same, flip


def join(same, flip):
    whole = in_order(lax.axis_index("ctx"), same, flip, 1)
    return pair(whole, "core", 0)


def shards(
    inputs,
    cotangent,
    segments,
    positions,
    attention_gain,
    attention_bias,
    joint_weight,
    joint_bias,
    output_weight,
    output_bias,
    feed_gain,
    feed_bias,
    up_weight,
    up_bias,
    down_weight,
    down_bias,
):
    section = lax.axis_index("section")
    count = inputs.shape[0]
    block = choose_columns(joint_weight[0], up_weight[0])
    pos = pair(pair(after(positions, block), "ctx", 2), "core", 1)
    seg = pair(after(segments, block), "core", 1)
    layer, whole_in, whole_grad = fetch_layer(
        block,
        (after(inputs, pos), cotangent),
        (
            attention_gain[0],
            attention_bias[0],
            joint_bias[0],
            output_bias[0],
            feed_gain[0],
            feed_bias[0],
            up_bias[0],
            down_bias[0],
        ),
        output_weight[0],
        down_weight[0],
    )
    layer = lax.optimization_barrier((*layer, whole_in, whole_grad))[:4]
    bias = layer[0][6]
    lane = jnp.arange(128) % HEAD_DIM
    rates = jnp.where(lane < ROT, 10000.0 ** (-2.0 * (lane % (ROT // 2)).astype(FULL) / ROT), 0.0)
    angle = pos.astype(FULL)[..., None] * rates
    cosine = jnp.cos(angle)
    sine = jnp.sin(angle) * jnp.where(lane < ROT // 2, -1.0, 1.0)
    places = [(seg[m][:, None, :], seg[m][:, :, None], cosine[m], sine[m]) for m in range(count)]
    c = lax.axis_index("ctx")
    k = lax.axis_index("core")

    def own_tokens(whole):
        return take(take(whole, k, 0).reshape(2, SEQ // 2, D), c, 0).astype(FULL)

    own_in = inputs[:, 0].astype(FULL) + bias
    (part,) = forward(whole_in[0], places[0], layer, False)
    own, give = sum_cores(part[None])
    (part,) = forward(after(whole_in[1], give), places[1], layer, False)
    result = (own_in[:1] + own + shift(give, "ctx", 1).astype(FULL)).astype(LOW)
    sent = [send_on(result, 0, 1)]
    own, give = sum_cores(after(part, result)[None])
    result = (own_in[1:] + own + shift(give, "ctx", 1).astype(FULL)).astype(LOW)
    sent.append(send_on(result, 0, 1))
    own_grad = cotangent[:, 0].astype(FULL)
    same, flip, _ = lax.optimization_barrier((*sent[0], result))
    hidden = [jnp.where(section == 0, whole_in[0], join(same, flip))]
    out_zero, *saved_zero = forward(hidden[0], places[0], layer, True)
    (part,) = backward(whole_grad[0], hidden[0], places[0], layer, saved_zero, False)
    own, give = sum_cores(part[None])
    same, flip, _ = lax.optimization_barrier((*sent[1], part))
    hidden.append(after(jnp.where(section == 0, whole_in[1], join(same, flip)), give))
    out_one, *saved_one = forward(hidden[1], places[1], layer, True)
    got = after(shift(give, "ctx", 1), out_one)
    result = (own_grad[:1] + own + got.astype(FULL)).astype(LOW)
    sent = [send_on(result, 1, 0)]
    (part,) = backward(
        after(whole_grad[1], result), hidden[1], places[1], layer, saved_one, False
    )
    own, give = sum_cores(part[None])
    same, flip, _ = lax.optimization_barrier((*sent[0], give))
    grad = jnp.where(section == 1, whole_grad[0], join(same, flip))
    result = (own_grad[1:] + own + shift(give, "ctx", 1).astype(FULL)).astype(LOW)
    sent.append(send_on(result, 1, 0))
    saved = [saved_zero, saved_one]
    grads = [after(grad, result)]

    def last(m):
        part, up_grad, joint_grad, sums = backward(
            grads[m], hidden[m], places[m], layer, saved[m], True
        )
        g = grads[m].reshape(-1, D)
        kept = saved[m]
        return part, (kept[0], kept[1], kept[6], g, joint_grad, up_grad), sums

    part_zero, factors_zero, sums_zero = last(0)
    same, flip, part_zero = lax.optimization_barrier((*sent[1], part_zero))
    grads.append(jnp.where(section == 1, whole_grad[1], join(same, flip)))
    (down,) = simple_call(
        down_kernel,
        "down_gradient",
        (saved_zero[7], grads[0].reshape(-1, D), saved_one[7], grads[1].reshape(-1, D)),
        [((FEED, D), LOW)],
    )
    down_share = lax.psum_scatter(down, ("y", "x"), scatter_dimension=0, tiled=True)
    parts = after(jnp.stack([out_zero, out_one, part_zero]), grads[1])
    grads[1] = after(grads[1], down)
    part_one, factors_one, sums_one = last(1)
    own_early, give = sum_cores(parts)
    grad_one = after(factors_one[3], give)
    one, two = simple_call(
        weights_kernel,
        "weight_gradients",
        (*factors_zero, *factors_one[:3], grad_one, *factors_one[4:]),
        [((D, SPLIT + LOCAL), LOW), ((D, FEED - SPLIT + 3 * LOCAL), LOW)],
    )
    joint_grad, out_grad, up_grad, down_grad, small, got, late = return_layer(
        one,
        two,
        down_share,
        sums_zero + sums_one,
        shift(give, "ctx", 1),
        over_cores(part_one[None]),
    )
    base = jnp.stack(
        [own_tokens(hidden[0]) + bias, own_tokens(hidden[1]) + bias, own_tokens(grads[0])]
    )
    early = (base + own_early + got.astype(FULL)).astype(LOW)
    late = (own_tokens(grads[1]) + late).astype(LOW)
    section_out = early[None, :2, None]
    input_grad = jnp.concatenate([early[2:], late])[None, :, None]
    return (
        section_out,
        input_grad,
        small[0],
        small[1],
        joint_grad,
        small[2],
        out_grad,
        small[3],
        small[4],
        small[5],
        up_grad,
        small[6],
        down_grad,
        small[7],
    )


def solution(mesh):
    finer = Mesh(mesh.devices.reshape(2, 2, 4, 4, 2), ("section", "ctx", "y", "x", "core"))
    fsdp = ("y", "x", "core")
    vector = P("section", fsdp)
    matrix = P("section", fsdp, None)
    tokens = P(None, fsdp, "ctx", None)
    kept = P("section", None, fsdp, "ctx", None)
    params = (
        vector,
        vector,
        matrix,
        vector,
        matrix,
        vector,
        vector,
        vector,
        matrix,
        vector,
        matrix,
        vector,
    )
    return jax.shard_map(
        shards,
        mesh=finer,
        in_specs=(tokens, tokens, P(None, fsdp, None), P(None, fsdp, "ctx")) + params,
        out_specs=(kept, kept) + params,
        check_vma=False,
    )
```

```python
import functools
import math

import jax
import jax.numpy as jnp
from jax import lax
from jax.experimental import pallas as pl
from jax.experimental.pallas import tpu as pltpu
from jax.sharding import Mesh
from jax.sharding import PartitionSpec as P

D = 1024
HEAD_DIM = 64
ROT = 16
SEQ = 256
LOCAL = 256
FEED = 1024
HERE = LOCAL // HEAD_DIM
EPSILON = 1e-05
LOW = jnp.bfloat16
FULL = jnp.float32
VMEM = 60 * 1024 * 1024


def shift(block, axis, distance):
    size = lax.axis_size(axis)
    return lax.ppermute(block, axis, [(i, (i + distance) % size) for i in range(size)])


def direct_blocks(block, axis):
    return [shift(block, axis, d) for d in (1, 2, 3)]


def stack_four(block, others, axis):
    me = lax.axis_index(axis)
    whole = jnp.zeros((4,) + block.shape, block.dtype)
    for distance, part in enumerate((block, *others)):
        whole = lax.dynamic_update_slice_in_dim(whole, part[None], (me - distance) % 4, 0)
    return whole


def shift_pair(block, axis, apart):
    size = lax.axis_size(axis)
    return lax.ppermute(block, axis, [(i, i ^ apart) for i in range(size)])


def quarter_of(block, dim, index):
    return lax.dynamic_index_in_dim(block, index % 4, dim, False)


def ring_start(block, axis, dim):
    far = quarter_of(block, dim, lax.axis_index(axis) + 2)
    cut = far.shape[-1] // 2
    return [shift(far[..., :cut], axis, 1), shift(far[..., cut:], axis, -1)]


def ring_next(block, axis, dim, up, down):
    me = lax.axis_index(axis)
    cut = up.shape[-1]
    ahead = quarter_of(block, dim, me + 1)
    behind = quarter_of(block, dim, me - 1)
    ahead = jnp.concatenate([plus(ahead[..., :cut], up), ahead[..., cut:]], -1)
    behind = jnp.concatenate([behind[..., :cut], plus(behind[..., cut:], down)], -1)
    return [shift(ahead, axis, 1), shift(behind, axis, -1)]


def direct(block, axis, dim):
    me = lax.axis_index(axis)
    return [shift(quarter_of(block, dim, me + d), axis, d) for d in (1, 3, 2)]


def together(*groups):
    flat = lax.optimization_barrier(tuple(item for group in groups for item in group))
    result = []
    for group in groups:
        result.append(flat[: len(group)])
        flat = flat[len(group) :]
    return result


def plus(*terms):
    return sum(term.astype(FULL) for term in terms).astype(LOW)


def after(block, *others):
    return lax.optimization_barrier((block,) + others)[0]


def in_order(index, own, other, dim):
    return jnp.where(
        index == 0,
        jnp.concatenate([own, other], dim),
        jnp.concatenate([other, own], dim),
    )


def pair(block, axis, dim):
    return in_order(lax.axis_index(axis), block, shift(block, axis, 1), dim)


def dot(left, right):
    return jnp.dot(left, right, preferred_element_type=FULL)


def dot_back(left, right):
    return lax.dot_general(left, right, (((1,), (1,)), ((), ())), preferred_element_type=FULL)


def dot_over(left, right):
    return lax.dot_general(left, right, (((0,), (0,)), ((), ())), preferred_element_type=FULL)


def turn(heads, cosine, sine):
    lane = lax.broadcasted_iota(jnp.int32, heads.shape, 1) % HEAD_DIM
    partner = jnp.where(
        lane < ROT // 2,
        pltpu.roll(heads, LOCAL - ROT // 2, 1),
        pltpu.roll(heads, ROT // 2, 1),
    )
    return heads * cosine + partner * sine


def normalize(hidden):
    centred = hidden - jnp.mean(hidden, -1, keepdims=True)
    scale = lax.rsqrt(jnp.mean(centred * centred, -1, keepdims=True) + EPSILON)
    return centred * scale, scale


def head_lanes(head):
    lane = lax.broadcasted_iota(jnp.int32, (SEQ, LOCAL), 1)
    return lane // HEAD_DIM == head


def head_stack(block):
    full = block.astype(FULL)
    copies = [jnp.where(head_lanes(head), full, 0.0) for head in range(HERE)]
    return jnp.concatenate(copies, 0).astype(LOW)


def head_pick(block):
    result = block[0]
    for head in range(1, HERE):
        result = jnp.where(head_lanes(head), block[head], result)
    return result


def by_head(block):
    return block.reshape(HERE, SEQ, SEQ)


def allowed_keys(seg_row, seg_col):
    query = lax.broadcasted_iota(jnp.int32, (SEQ, SEQ), 0)
    key = lax.broadcasted_iota(jnp.int32, (SEQ, SEQ), 1)
    return (seg_col == seg_row) & (query >= key)


def forward_kernel(keep, load, out, store):
    hidden, seg_row, seg_col, cosine, sine, params, w_joint, w_out, w_up, w_down = load
    normed, _ = normalize(hidden()[...].astype(FULL))
    params = params()
    first = (normed * params[0:1] + params[1:2]).astype(LOW)
    second = (normed * params[2:3] + params[3:4]).astype(LOW)
    if keep:
        out[2][...] = first
        out[3][...] = second
        store(2, 3)
    cos = jnp.concatenate([cosine()[...]] * 2, 1)
    sin = jnp.concatenate([sine()[...]] * 2, 1)
    joint = dot(first, w_joint()[...]) + params[4:5, : 3 * LOCAL]
    query = turn(joint[:, :LOCAL], cos, sin)
    keys = turn(joint[:, LOCAL : 2 * LOCAL], cos, sin).astype(LOW)
    values = joint[:, 2 * LOCAL :].astype(LOW)
    if keep:
        out[4][...] = query.astype(LOW)
        out[5][...] = keys
        out[6][...] = values
        store(4, 5, 6)
    contexts = []
    for seq in range(2):
        part = slice(seq * SEQ, seq * SEQ + SEQ)
        scores = by_head(dot_back(head_stack(query[part]), keys[part]))
        scores = jnp.where(
            allowed_keys(seg_row()[seq], seg_col()[seq])[None],
            scores * HEAD_DIM**-0.5,
            -1000000000.0,
        )
        top = jnp.max(scores, -1, keepdims=True)
        weight = jnp.exp(scores - top)
        total = jnp.sum(weight, -1, keepdims=True)
        probs = (weight * (1.0 / total)).astype(LOW).reshape(HERE * SEQ, SEQ)
        contexts.append(head_pick(by_head(dot(probs, values[part]))).astype(LOW))
        if keep:
            out[7][pl.ds(seq * HERE, HERE)] = top + jnp.log(total)
    context = jnp.concatenate(contexts, 0)
    if keep:
        out[8][...] = context
        store(7, 8)
    upward = dot(second, w_up()[...]) + params[5:6]
    half = 0.5 * (1.0 + lax.erf(upward * math.sqrt(0.5)))
    active = (upward * half).astype(LOW)
    if keep:
        out[9][...] = active
        slope = half + upward * jnp.exp(-0.5 * upward * upward) * math.sqrt(0.5 / math.pi)
        out[10][...] = slope.astype(LOW)
        store(9, 10)
    result = (dot(context, w_out()[:, :D]) + dot(active, w_down()[...])).astype(LOW)
    out[0][...] = result[:SEQ]
    out[1][...] = result[SEQ:]
    store(0, 1)


def backward_kernel(keep, load, out, store):
    (grad, w_out, seg_row, seg_col, query_in, keys_in, values_in, lse_in) = load[:8]
    (cosine, sine, params, w_joint, w_down, slope, w_up, hidden) = load[8:]
    g = grad()[...]
    context_grad = dot_back(g, w_out()[:, :D])
    turned = []
    for seq in range(2):
        part = slice(seq * SEQ, seq * SEQ + SEQ)
        query = query_in()[part]
        keys = keys_in()[part]
        values = values_in()[part]
        queries = head_stack(query)
        contexts = head_stack(context_grad[part])
        scores = by_head(dot_back(queries, keys))
        scores = jnp.where(
            allowed_keys(seg_row()[seq], seg_col()[seq])[None],
            scores * HEAD_DIM**-0.5,
            -1000000000.0,
        )
        probs = jnp.exp(scores - lse_in()[pl.ds(seq * HERE, HERE)])
        probs_grad = by_head(dot_back(contexts, values))
        scores_grad = probs * (probs_grad - jnp.sum(probs * probs_grad, -1, keepdims=True))
        scores_grad = scores_grad.astype(LOW).reshape(HERE * SEQ, SEQ)
        probs = probs.astype(LOW).reshape(HERE * SEQ, SEQ)
        query_grad = head_pick(by_head(dot(scores_grad, keys)))
        keys_grad = dot_over(scores_grad, queries)
        values_grad = dot_over(probs, contexts)
        cos = jnp.concatenate([cosine()[part]] * 2, 1)
        sin = -jnp.concatenate([sine()[part]] * 2, 1)
        turned.append(
            jnp.concatenate(
                [
                    turn(query_grad * HEAD_DIM**-0.5, cos, sin),
                    turn(keys_grad * HEAD_DIM**-0.5, cos, sin),
                    values_grad,
                ],
                1,
            ).astype(LOW)
        )
    joint_grad = jnp.concatenate(turned, 0)
    if keep:
        out[3][...] = joint_grad
        store(3)
    first_grad = dot_back(joint_grad, w_joint()[...])
    up_grad = dot_back(g, w_down()[...]) * slope()[...].astype(FULL)
    up_grad = up_grad.astype(LOW)
    if keep:
        out[2][...] = up_grad
        store(2)
    second_grad = dot_back(up_grad, w_up()[...])
    normed, scale = normalize(hidden()[...].astype(FULL))
    params = params()
    inner = first_grad * params[0:1] + second_grad * params[2:3]
    back = scale * (
        inner
        - jnp.mean(inner, -1, keepdims=True)
        - normed * jnp.mean(inner * normed, -1, keepdims=True)
    )
    result = back.astype(LOW)
    out[0][...] = result[:SEQ]
    out[1][...] = result[SEQ:]
    store(0, 1)
    if keep:
        out[4][...] = jnp.zeros(out[4].shape, FULL)
        for row, item in (
            (0, first_grad * normed),
            (1, first_grad),
            (2, second_grad * normed),
            (3, second_grad),
            (4, up_grad.astype(FULL)),
            (5, g.astype(FULL)),
            (6, joint_grad.astype(FULL)),
        ):
            out[4][row : row + 1, : item.shape[1]] = jnp.sum(item, 0, keepdims=True)
        store(4)


JOINT = slice(0, 3 * LOCAL)
UP = slice(3 * LOCAL, 3 * LOCAL + FEED)
DOWN = slice(3 * LOCAL + FEED, 3 * LOCAL + FEED + D)
TOKENS = 2 * SEQ


class Pieces:
    def __init__(self, refs):
        self.refs = refs

    def __getitem__(self, index):
        return jnp.concatenate([ref[...] for ref in self.refs], 0)[index]


def call(kernel, name, operands, shapes, flops):
    arrays = []

    def number(array):
        for place, item in enumerate(arrays):
            if item is array:
                return place
        arrays.append(array)
        return len(arrays) - 1

    views = []
    for operand in operands:
        if isinstance(operand[-1], slice):
            views.append((number(operand[0]), operand[1]))
        else:
            views.append([number(array) for array in operand])

    def body(*refs):
        sources, results = refs[: len(arrays)], refs[len(arrays) :]

        def loader(view):
            if isinstance(view, tuple):
                return lambda: sources[view[0]].at[:, view[1]]
            if len(view) == 1:
                return lambda: sources[view[0]]
            return lambda: Pieces([sources[place] for place in view])

        kernel([loader(view) for view in views], results, lambda *numbers: None)

    return pl.pallas_call(
        body,
        in_specs=[pl.BlockSpec(memory_space=pltpu.VMEM)] * len(arrays),
        out_specs=[pl.BlockSpec(memory_space=pltpu.VMEM)] * len(shapes),
        out_shape=[jax.ShapeDtypeStruct(shape, kind) for shape, kind in shapes],
        compiler_params=pltpu.CompilerParams(vmem_limit_bytes=20 * 1024 * 1024),
        cost_estimate=pl.CostEstimate(flops=flops, bytes_accessed=8 * D * D, transcendentals=0),
        name=name,
    )(*arrays)


def own_call(kernel, name, operands, shapes, flops):
    arrays = []
    parts = []
    held = []
    for operand in operands:
        if isinstance(operand[-1], slice):
            array, columns = operand
            parts.append([(len(arrays), columns, None)])
            arrays.append(array)
            held.append(((array.shape[0], columns.stop - columns.start), array.dtype))
        else:
            row = 0
            pieces = []
            for array in operand:
                whole = None if len(operand) == 1 else pl.ds(row, array.shape[0])
                pieces.append((len(arrays), None, whole))
                arrays.append(array)
                row += array.shape[0]
            parts.append(pieces)
            held.append(((row,) + operand[0].shape[1:], operand[0].dtype))

    def body(*refs):
        sources, refs = refs[: len(arrays)], refs[len(arrays) :]
        results, refs = refs[: len(shapes)], refs[len(shapes) :]
        near, refs = refs[: len(held)], refs[len(held) :]
        kept, (come, go) = refs[: len(shapes)], refs[len(shapes) :]
        copies = []
        for pieces, ref in zip(parts, near):
            group = []
            for index, columns, place in pieces:
                source = sources[index] if columns is None else sources[index].at[:, columns]
                target = ref if place is None else ref.at[place]
                group.append(pltpu.make_async_copy(source, target, come.at[index]))
                group[-1].start()
            copies.append(group)
        done = set()

        def loader(number):
            def load():
                if number not in done:
                    done.add(number)
                    for copy in copies[number]:
                        copy.wait()
                return near[number]

            return load

        sent = []

        def store(*numbers):
            for number in numbers:
                copy = pltpu.make_async_copy(kept[number], results[number], go.at[number])
                copy.start()
                sent.append(copy)

        loaders = [loader(number) for number in range(len(held))]
        kernel(loaders, kept, store)
        for load in loaders:
            load()
        for copy in sent:
            copy.wait()

    return pl.pallas_call(
        body,
        in_specs=[pl.BlockSpec(memory_space=pltpu.HBM)] * len(arrays),
        out_specs=[pl.BlockSpec(memory_space=pltpu.HBM)] * len(shapes),
        out_shape=[jax.ShapeDtypeStruct(shape, kind) for shape, kind in shapes],
        scratch_shapes=[pltpu.VMEM(shape, kind) for shape, kind in held]
        + [pltpu.VMEM(shape, kind) for shape, kind in shapes]
        + [pltpu.SemaphoreType.DMA((len(arrays),)), pltpu.SemaphoreType.DMA((len(shapes),))],
        compiler_params=pltpu.CompilerParams(vmem_limit_bytes=VMEM),
        cost_estimate=pl.CostEstimate(flops=flops, bytes_accessed=8 * D * D, transcendentals=0),
        name=name,
    )(*arrays)


ESTIMATE = TOKENS * 16 * D * D
HALVES = [((SEQ, D), LOW)] * 2


def forward(hidden, place, layer, keep):
    seg_row, seg_col, cosine, sine = ((item,) for item in place)
    params, weights, w_out = layer
    shapes = list(HALVES)
    if keep:
        wide = ((TOKENS, D), LOW)
        narrow = ((TOKENS, LOCAL), LOW)
        lse = ((2 * HERE, SEQ, 1), FULL)
        shapes += [wide, wide, narrow, narrow, narrow, lse, narrow, wide, wide]
    operands = (
        hidden,
        seg_row,
        seg_col,
        cosine,
        sine,
        (params,),
        (weights, JOINT),
        (w_out,),
        (weights, UP),
        (weights, DOWN),
    )
    kernel = functools.partial(forward_kernel, keep)
    return call(kernel, "layer_forward", operands, shapes, ESTIMATE)


def backward(grad, hidden, place, layer, saved, keep):
    seg_row, seg_col, cosine, sine = ((item,) for item in place)
    params, weights, w_out = layer
    shapes = list(HALVES)
    if keep:
        shapes += [((TOKENS, FEED), LOW), ((TOKENS, 3 * LOCAL), LOW), ((8, D), FULL)]
    operands = (
        grad,
        (w_out,),
        seg_row,
        seg_col,
        *((item,) for item in saved[2:6]),
        cosine,
        sine,
        (params,),
        (weights, JOINT),
        (weights, DOWN),
        (saved[8],),
        (weights, UP),
        hidden,
    )
    kernel = functools.partial(backward_kernel, keep)
    return call(kernel, "layer_backward", operands, shapes, ESTIMATE)


def lower_upper(lower, upper, half):
    lane = lax.broadcasted_iota(jnp.int32, lower.shape, 1)
    if half == 0:
        return jnp.where(lane < HEAD_DIM, lower, pltpu.roll(upper, HEAD_DIM, 1))
    return jnp.where(lane < HEAD_DIM, pltpu.roll(lower, HEAD_DIM, 1), upper)


def choose_kernel(place, joint, up, out):
    c, k = place[0], place[1]

    def group(ref, index):
        return ref[:, pl.ds(pl.multiple_of(index * 128, 128), 128)].astype(FULL)

    for pair_ in range(6):
        lower = group(joint, 4 * pair_ + c)
        upper = group(joint, 4 * pair_ + 2 + c)
        here = slice(pair_ * 128, pair_ * 128 + 128)
        out[k, :, here] = lower_upper(lower, upper, 0).astype(LOW)
        out[1 - k, :, here] = lower_upper(lower, upper, 1).astype(LOW)
    for pair_ in range(8):
        here = slice(3 * LOCAL + pair_ * 128, 3 * LOCAL + pair_ * 128 + 128)
        for slot, core in ((0, k), (1, 1 - k)):
            lower = group(up, 4 * pair_ + core)
            upper = group(up, 4 * pair_ + 2 + core)
            block = jnp.where(
                jnp.zeros(lower.shape, jnp.int32) + c == 0,
                lower_upper(lower, upper, 0),
                lower_upper(lower, upper, 1),
            )
            out[slot, :, here] = block.astype(LOW)


def finish_kernel(
    place, block, down_in, out_own, out_other, sums, joint, out, up, down, *rest
):
    vectors, (whole, up_all, joint_all) = rest[:8], rest[8:]

    def quarter(c, k, column):
        return block[c, 32 * k : 32 * k + 32, column : column + 128].astype(FULL)

    def vector(c, k, column):
        return sums[2 * c + k, :, column : column + 128]

    for p in range(16):
        at = p // 2 * 128
        for k in range(2):
            here = slice((2 * p + k) * 128, (2 * p + k) * 128 + 128)
            up[0, :, here] = lower_upper(quarter(0, k, at), quarter(1, k, at), p % 2)
            up_all[:, here] = lower_upper(vector(0, k, at), vector(1, k, at), p % 2)
    for t in range(12):
        at = t // 2 * 128
        for c in range(2):
            here = slice((2 * t + c) * 128, (2 * t + c) * 128 + 128)
            joint[0, :, here] = lower_upper(
                quarter(c, 0, FEED + at), quarter(c, 1, FEED + at), t % 2
            )
            joint_all[:, here] = lower_upper(vector(c, 0, at), vector(c, 1, at), t % 2)
    joint_all[:, 3 * D :] = jnp.zeros((8, 128), FULL)
    for c in range(2):
        down[0, 64 * c : 64 * c + 64] = down_in[c].astype(FULL)
    out[0] = out_own[...].astype(FULL) + out_other[...].astype(FULL)
    whole[...] = sums[0] + sums[1] + sums[2] + sums[3]
    whole[5:6] = sums[0, 5:6]
    f = place[0]

    def lanes(ref, start, width):
        first = pl.multiple_of(start // 128 * 128, 128)
        return pltpu.roll(ref[:, pl.ds(first, width)], (width - start % 128) % width, 1)

    shares = lanes(whole, f * 32, 128)
    for index, row in ((0, 0), (1, 1), (3, 5), (4, 2), (5, 3), (7, 5)):
        vectors[index][...] = shares[row : row + 1, :32]
    vectors[2][...] = lanes(joint_all, f * 96, 256)[6:7, :96]
    vectors[6][...] = up_all[4:5, pl.ds(pl.multiple_of(f * 128, 128), 128)]


def down_kernel(load, out, store):
    active, grad = load
    out[0][...] = dot_over(active()[...], grad()[...]).astype(LOW)
    store(0)


def weights_kernel(load, out, store):
    second, up_grad, context, grad, first, joint_grad = load
    one, two = out
    up = dot_over(second()[...], up_grad()[...]).astype(LOW)
    one[:, :SPLIT] = up[:, :SPLIT]
    two[:, : FEED - SPLIT] = up[:, SPLIT:]
    term = dot_over(context()[...], grad()[...]).astype(LOW)
    for y in range(4):
        for x in range(4):
            rows = slice((4 * y + x) * 64, (4 * y + x) * 64 + 64)
            one[rows, SPLIT:] = term[64 * y : 64 * y + 64, LOCAL * x : LOCAL * x + LOCAL]
    store(0)
    two[:, FEED - SPLIT :] = dot_over(first()[...], joint_grad()[...]).astype(LOW)
    store(1)


SPLIT = 768


def simple_call(kernel, name, operands, shapes, scalars=0, scratch=()):
    return pl.pallas_call(
        kernel,
        in_specs=[pl.BlockSpec(memory_space=pltpu.SMEM)] * scalars
        + [pl.BlockSpec(memory_space=pltpu.VMEM)] * (len(operands) - scalars),
        out_specs=[pl.BlockSpec(memory_space=pltpu.VMEM)] * len(shapes),
        out_shape=[jax.ShapeDtypeStruct(shape, kind) for shape, kind in shapes],
        scratch_shapes=[pltpu.VMEM(shape, FULL) for shape in scratch],
        compiler_params=pltpu.CompilerParams(vmem_limit_bytes=24 * 1024 * 1024),
        name=name,
    )(*operands)


SMALL = (32, 32, 96, 32, 32, 32, 128, 32)
EDGES = [sum(SMALL[:i]) for i in range(len(SMALL) + 1)]


def choose_columns(joint_weight, up_weight):
    c = lax.axis_index("ctx")
    k = lax.axis_index("core")
    (chosen,) = simple_call(
        choose_kernel,
        "choose_columns",
        (jnp.stack([c, k]), joint_weight, up_weight),
        [((2, 32, 3 * LOCAL + FEED), LOW)],
        1,
    )
    return in_order(k, chosen[0], shift(chosen[1], "core", 1), 0)


def fetch_layer(block, tokens, small, output_weight, down_weight):
    c = lax.axis_index("ctx")
    k = lax.axis_index("core")
    quarter = 2 * c + k
    down = lax.dynamic_slice_in_dim(down_weight, c * 64, 64, 0)
    block = jnp.concatenate([block, down], 1)
    weights = lax.all_gather(block, ("y", "x"), axis=0, tiled=True)
    vectors = jnp.concatenate(small + (jnp.zeros((512 - sum(SMALL),), LOW),)).reshape(4, 128)
    vectors = jnp.concatenate([vectors, jnp.zeros((28, 128), LOW)], 0)
    mixed = pair(after(jnp.concatenate([output_weight, vectors], 1), block), "core", 0)
    others, (got,) = together(direct_blocks(mixed, "x"), [shift(tokens[0], "ctx", 1)])
    later, got = lax.optimization_barrier((tokens[1], got))
    inputs = in_order(c, tokens[0], got, 1)
    mixed = stack_four(mixed, others, "x")
    out = lax.dynamic_index_in_dim(mixed, quarter, 0, False)[:, :D]
    vectors = mixed[:, :, D:].reshape(4, 2, 32, 128)[:, :, :8].reshape(64, 128)
    out = jnp.concatenate([out, vectors], 1)
    others, (inputs_other, got) = together(
        direct_blocks(out, "y"), [shift(inputs, "core", 1), shift(later, "ctx", 1)]
    )
    cotangent = in_order(c, later, got, 1)
    out = stack_four(out, others, "y")
    inputs = (inputs, inputs_other)
    cotangent = (cotangent, shift(cotangent, "core", 1))
    vectors = out[:, :, D:].reshape(32, 8, 128)[:, :4].reshape(32, 512)
    small = [vectors[:, a:b].reshape(-1).astype(FULL) for a, b in zip(EDGES, EDGES[1:])]
    joint_bias = lax.dynamic_index_in_dim(
        small[2].reshape(3, 4, 4, HEAD_DIM), quarter, 2, False
    ).reshape(-1)
    up_bias = small[6].reshape(16, 2, 2, HEAD_DIM)
    up_bias = lax.dynamic_index_in_dim(
        lax.dynamic_index_in_dim(up_bias, c, 2, False), k, 1, False
    ).reshape(-1)
    params = jnp.stack(
        [
            small[0],
            small[1],
            small[4],
            small[5],
            jnp.pad(joint_bias, (0, D - 3 * LOCAL)),
            up_bias,
            small[3] + small[7],
            jnp.zeros((D,), FULL),
        ]
    )
    layer = (params, weights, out.reshape(LOCAL, D + 128))
    return layer, inputs, cotangent


def return_layer(one, two, down, sums, beside, late):
    c = lax.axis_index("ctx")
    k = lax.axis_index("core")
    x = lax.axis_index("x")
    y = lax.axis_index("y")
    one = one.reshape(4, 4, 64, -1)
    two = two.reshape(4, 4, 64, -1)
    sums = sums + shift_pair(sums, "y", 1)
    ones, twos, (more, beside, core) = together(
        ring_start(one, "y", 0),
        ring_start(two, "x", 1),
        [shift_pair(sums, "y", 2), beside, late[1]],
    )
    sums = sums + more
    own, give = halves_of(late[0], core)
    ones, twos, (more, got) = together(
        ring_next(one, "y", 0, *ones),
        ring_next(two, "x", 1, *twos),
        [shift_pair(sums, "x", 1), shift(give, "ctx", 1)],
    )
    sums = sums + more
    one = plus(quarter_of(one, 0, y), *ones)
    two = plus(quarter_of(two, 1, x), *twos)
    out = one[:, :, SPLIT :].transpose(1, 0, 2).reshape(1, 64, D)
    out = jnp.where(
        jnp.arange(4)[:, None, None] == 2 * c + k, out, jnp.zeros_like(out)
    )
    one = jnp.concatenate([one[:, :, : SPLIT], out], -1)
    ones, twos, (more, down_more) = together(
        direct(one, "x", 0),
        direct(two, "y", 0),
        [shift_pair(sums, "x", 2), shift(down, "ctx", 1)],
    )
    sums = sums + more
    one = plus(quarter_of(one, 0, x), *ones)
    two = plus(quarter_of(two, 0, y), *twos)
    both = jnp.concatenate([one[:, :SPLIT], two, one[:, SPLIT:]], 1)
    both = both.reshape(2, 32, -1)
    width = FEED + 3 * LOCAL
    mine = take(both, k, 0)
    (other,), (more,) = together(
        [shift(take(both, 1 - k, 0), "core", 1)], [shift(sums, "core", 1)]
    )
    sums = in_order(k, sums[None], more[None], 0)
    block = in_order(k, mine[:, :width], other[:, :width], 0)
    out = plus(mine[:, width:], other[:, width:])
    (block_more, out_more, sums_more), _ = together(
        [shift(block, "ctx", 1), shift(out, "ctx", 1), shift(sums, "ctx", 1)], [beside]
    )
    place = (4 * y + x) * 2 + k
    vectors = [((1, width), FULL) for width in SMALL]
    joint, out, up, down, *vectors = simple_call(
        finish_kernel,
        "finish",
        (
            place[None],
            in_order(c, block[None], block_more[None], 0),
            in_order(c, down[None], down_more[None], 0),
            out,
            out_more,
            in_order(c, sums, sums_more, 0),
        ),
        [((1, 32, 3 * D), FULL), ((1, 32, D), FULL), ((1, 32, 4 * D), FULL), ((1, 128, D), FULL)]
        + vectors,
        1,
        ((8, D), (8, 4 * D), (8, 3 * D + 128)),
    )
    return joint, out, up, down, vectors, beside, own + got.astype(FULL)


def plus_full(left, right):
    return left.astype(FULL) + right.astype(FULL)


def take(block, index, dim):
    return lax.dynamic_index_in_dim(block, index, dim, False)


def halves_of(mine, other):
    c = lax.axis_index("ctx")
    total = plus_full(mine, other)
    total = total.reshape(total.shape[:-2] + (2, SEQ // 2, D))
    dim = total.ndim - 3
    return take(total, c, dim), take(total, 1 - c, dim).astype(LOW)


def sum_cores(mine, other):
    return halves_of(mine, shift(other, "core", 1))


def send_on(block):
    same = lax.ppermute(block, ("section", "ctx"), [(i, (i + 2) % 4) for i in range(4)])
    flip = lax.ppermute(block, ("section", "ctx"), [(i, 3 - i) for i in range(4)])
    return same, flip


def join(keep, whole, same, flip):
    mine = jnp.where(keep, whole, in_order(lax.axis_index("ctx"), same, flip, 0))
    return mine, shift(mine, "core", 1)


def split_two(results):
    return results[0], results[1], results[2:]


def shards(
    inputs,
    cotangent,
    segments,
    positions,
    attention_gain,
    attention_bias,
    joint_weight,
    joint_bias,
    output_weight,
    output_bias,
    feed_gain,
    feed_bias,
    up_weight,
    up_bias,
    down_weight,
    down_bias,
):
    section = lax.axis_index("section")
    count = inputs.shape[0]
    block = choose_columns(joint_weight[0], up_weight[0])
    pos = pair(after(positions[:, 0], block), "ctx", 1)
    pos = jnp.stack([pos, shift(pos, "core", 1)], 1)
    seg = after(segments[:, 0], block)
    seg = jnp.stack([seg, shift(seg, "core", 1)], 1)
    early, pos, seg = lax.optimization_barrier((inputs[:, 0], pos, seg))
    layer, whole_in, whole_grad = fetch_layer(
        block,
        (early, cotangent[:, 0]),
        (
            attention_gain[0],
            attention_bias[0],
            joint_bias[0],
            output_bias[0],
            feed_gain[0],
            feed_bias[0],
            up_bias[0],
            down_bias[0],
        ),
        output_weight[0],
        down_weight[0],
    )
    bias = layer[0][6]
    lane = jnp.arange(128) % HEAD_DIM
    rates = jnp.where(lane < ROT, 10000.0 ** (-2.0 * (lane % (ROT // 2)).astype(FULL) / ROT), 0.0)
    angle = pos.astype(FULL)[..., None] * rates
    cosine = jnp.cos(angle).reshape(count, TOKENS, 128)
    sine = (jnp.sin(angle) * jnp.where(lane < ROT // 2, -1.0, 1.0)).reshape(count, TOKENS, 128)
    places = [(seg[m][:, None, :], seg[m][:, :, None], cosine[m], sine[m]) for m in range(count)]
    c = lax.axis_index("ctx")

    def of(pair_, m):
        return tuple(item[m] for item in pair_)

    def own_tokens(whole):
        return take(whole.reshape(2, SEQ // 2, D), c, 0).astype(FULL)

    def over_ctx(base, own, give):
        return (base + own + shift(give, "ctx", 1).astype(FULL)).astype(LOW)

    own_in = inputs[:, 0].astype(FULL) + bias
    part = forward(of(whole_in, 0), places[0], layer, False)
    own, give = sum_cores(*part)
    a, b = of(whole_in, 1)
    part = forward((after(a, give), b), places[1], layer, False)
    result = over_ctx(own_in[0], own, give)
    sent = [send_on(result)]
    own, give = sum_cores(part[0], after(part[1], result))
    result = over_ctx(own_in[1], own, give)
    sent.append(send_on(result))
    own_grad = cotangent[:, 0].astype(FULL)
    same, flip, _ = lax.optimization_barrier((*sent[0], result))
    hidden = [join(section == 0, whole_in[0][0], same, flip)]
    *out_zero, saved_zero = split_two(forward(hidden[0], places[0], layer, True))
    part = backward(of(whole_grad, 0), hidden[0], places[0], layer, saved_zero, False)
    own, give = sum_cores(*part)
    same, flip, _ = lax.optimization_barrier((*sent[1], part[0]))
    a, b = join(section == 0, whole_in[0][1], same, flip)
    hidden.append((a, after(b, give)))
    *out_one, saved_one = split_two(forward(hidden[1], places[1], layer, True))
    got = after(shift(give, "ctx", 1), out_one[0])
    result = (own_grad[0] + own + got.astype(FULL)).astype(LOW)
    sent = [send_on(result)]
    a, b = of(whole_grad, 1)
    part = backward((after(a, result), b), hidden[1], places[1], layer, saved_one, False)
    same, flip, *part = lax.optimization_barrier((*sent[0], *part))
    a, b = join(section == 1, whole_grad[0][0], same, flip)
    own, give = sum_cores(*part)
    result = over_ctx(own_grad[1], own, give)
    sent.append(send_on(result))
    saved = [saved_zero, saved_one]
    grads = [(a, after(b, result))]

    def last(m):
        return backward(grads[m], hidden[m], places[m], layer, saved[m], True)

    *part_zero, up_zero, joint_zero, sums_zero = last(0)
    same, flip, part_zero[0] = lax.optimization_barrier((*sent[1], part_zero[0]))
    grads.append(join(section == 1, whole_grad[0][1], same, flip))
    both = (*grads[0], *grads[1])
    (down,) = call(
        down_kernel,
        "down_gradient",
        ((saved_zero[7], saved_one[7]), both),
        [((FEED, D), LOW)],
        2 * TOKENS * 4 * D * D,
    )
    down_share = lax.psum_scatter(down, ("y", "x"), scatter_dimension=0, tiled=True)
    ready = grads[1][1]
    outs = [
        jnp.stack([out_zero[i], out_one[i], after(part_zero[i], ready)]) for i in range(2)
    ]
    grads[1] = (grads[1][0], after(grads[1][1], down))
    *part_one, up_one, joint_one, sums_one = last(1)
    own_early, give = sum_cores(*outs)
    one, two = own_call(
        weights_kernel,
        "weight_gradients",
        (
            (saved_zero[1], saved_one[1]),
            (up_zero, up_one),
            (saved_zero[6], saved_one[6]),
            (after(both[0], give), *both[1:]),
            (saved_zero[0], saved_one[0]),
            (joint_zero, joint_one),
        ),
        [((D, SPLIT + LOCAL), LOW), ((D, FEED - SPLIT + 3 * LOCAL), LOW)],
        2 * TOKENS * 8 * D * D,
    )
    joint_grad, out_grad, up_grad, down_grad, small, got, late = return_layer(
        one,
        two,
        down_share,
        sums_zero + sums_one,
        shift(give, "ctx", 1),
        (part_one[0], shift(part_one[1], "core", 1)),
    )
    base = jnp.stack(
        [own_tokens(hidden[0][0]) + bias, own_tokens(hidden[1][0]) + bias, own_tokens(grads[0][0])]
    )
    early = (base + own_early + got.astype(FULL)).astype(LOW)
    late = (own_tokens(grads[1][0])[None] + late).astype(LOW)
    section_out = early[None, :2, None]
    input_grad = jnp.concatenate([early[2:], late])[None, :, None]
    return (
        section_out,
        input_grad,
        small[0],
        small[1],
        joint_grad,
        small[2],
        out_grad,
        small[3],
        small[4],
        small[5],
        up_grad,
        small[6],
        down_grad,
        small[7],
    )


def solution(mesh):
    finer = Mesh(mesh.devices.reshape(2, 2, 4, 4, 2), ("section", "ctx", "y", "x", "core"))
    fsdp = ("y", "x", "core")
    vector = P("section", fsdp)
    matrix = P("section", fsdp, None)
    tokens = P(None, fsdp, "ctx", None)
    kept = P("section", None, fsdp, "ctx", None)
    params = (
        vector,
        vector,
        matrix,
        vector,
        matrix,
        vector,
        vector,
        vector,
        matrix,
        vector,
        matrix,
        vector,
    )
    return jax.shard_map(
        shards,
        mesh=finer,
        in_specs=(tokens, tokens, P(None, fsdp, None), P(None, fsdp, "ctx")) + params,
        out_specs=(kept, kept) + params,
        check_vma=False,
    )
```

```python
import functools
import math

import jax
import jax.numpy as jnp
from jax import lax
from jax.experimental import pallas as pl
from jax.experimental.pallas import tpu as pltpu
from jax.sharding import Mesh
from jax.sharding import PartitionSpec as P

D = 1024
HEAD_DIM = 64
ROT = 16
SEQ = 256
LOCAL = 256
FEED = 1024
HERE = LOCAL // HEAD_DIM
EPSILON = 1e-05
LOW = jnp.bfloat16
FULL = jnp.float32
VMEM = 60 * 1024 * 1024


def shift(block, axis, distance):
    size = lax.axis_size(axis)
    return lax.ppermute(block, axis, [(i, (i + distance) % size) for i in range(size)])


def direct_blocks(block, axis):
    return [shift(block, axis, d) for d in (1, 2, 3)]


def stack_four(block, others, axis):
    me = lax.axis_index(axis)
    whole = jnp.zeros((4,) + block.shape, block.dtype)
    for distance, part in enumerate((block, *others)):
        whole = lax.dynamic_update_slice_in_dim(whole, part[None], (me - distance) % 4, 0)
    return whole


def shift_pair(block, axis, apart):
    size = lax.axis_size(axis)
    return lax.ppermute(block, axis, [(i, i ^ apart) for i in range(size)])


def quarter_of(block, dim, index):
    return lax.dynamic_index_in_dim(block, index % 4, dim, False)


def ring_start(block, axis, dim):
    far = quarter_of(block, dim, lax.axis_index(axis) + 2)
    cut = far.shape[-1] // 2
    return [shift(far[..., :cut], axis, 1), shift(far[..., cut:], axis, -1)]


def ring_next(block, axis, dim, up, down):
    me = lax.axis_index(axis)
    cut = up.shape[-1]
    ahead = quarter_of(block, dim, me + 1)
    behind = quarter_of(block, dim, me - 1)
    ahead = jnp.concatenate([plus(ahead[..., :cut], up), ahead[..., cut:]], -1)
    behind = jnp.concatenate([behind[..., :cut], plus(behind[..., cut:], down)], -1)
    return [shift(ahead, axis, 1), shift(behind, axis, -1)]


def direct(block, axis, dim):
    me = lax.axis_index(axis)
    return [shift(quarter_of(block, dim, me + d), axis, d) for d in (1, 3, 2)]


def together(*groups):
    flat = lax.optimization_barrier(tuple(item for group in groups for item in group))
    result = []
    for group in groups:
        result.append(flat[: len(group)])
        flat = flat[len(group) :]
    return result


def plus(*terms):
    return sum(term.astype(FULL) for term in terms).astype(LOW)


def after(block, *others):
    return lax.optimization_barrier((block,) + others)[0]


def in_order(index, own, other, dim):
    return jnp.where(
        index == 0,
        jnp.concatenate([own, other], dim),
        jnp.concatenate([other, own], dim),
    )


def pair(block, axis, dim):
    return in_order(lax.axis_index(axis), block, shift(block, axis, 1), dim)


def dot(left, right):
    return jnp.dot(left, right, preferred_element_type=FULL)


def dot_back(left, right):
    return lax.dot_general(left, right, (((1,), (1,)), ((), ())), preferred_element_type=FULL)


def dot_over(left, right):
    return lax.dot_general(left, right, (((0,), (0,)), ((), ())), preferred_element_type=FULL)


def turn(heads, cosine, sine):
    lane = lax.broadcasted_iota(jnp.int32, heads.shape, 1) % HEAD_DIM
    partner = jnp.where(
        lane < ROT // 2,
        pltpu.roll(heads, LOCAL - ROT // 2, 1),
        pltpu.roll(heads, ROT // 2, 1),
    )
    return heads * cosine + partner * sine


def normalize(hidden):
    centred = hidden - jnp.mean(hidden, -1, keepdims=True)
    scale = lax.rsqrt(jnp.mean(centred * centred, -1, keepdims=True) + EPSILON)
    return centred * scale, scale


def head_lanes(head):
    lane = lax.broadcasted_iota(jnp.int32, (SEQ, LOCAL), 1)
    return lane // HEAD_DIM == head


def head_stack(block):
    full = block.astype(FULL)
    copies = [jnp.where(head_lanes(head), full, 0.0) for head in range(HERE)]
    return jnp.concatenate(copies, 0).astype(LOW)


def head_pick(block):
    result = block[0]
    for head in range(1, HERE):
        result = jnp.where(head_lanes(head), block[head], result)
    return result


def by_head(block):
    return block.reshape(HERE, SEQ, SEQ)


def allowed_keys(seg_row, seg_col):
    query = lax.broadcasted_iota(jnp.int32, (SEQ, SEQ), 0)
    key = lax.broadcasted_iota(jnp.int32, (SEQ, SEQ), 1)
    return (seg_col == seg_row) & (query >= key)


def forward_kernel(keep, load, out, store):
    hidden, seg_row, seg_col, cosine, sine, params, w_joint, w_out, w_up, w_down = load
    normed, _ = normalize(hidden()[...].astype(FULL))
    params = params()
    first = (normed * params[0:1] + params[1:2]).astype(LOW)
    second = (normed * params[2:3] + params[3:4]).astype(LOW)
    if keep:
        out[2][...] = first
        out[3][...] = second
        store(2, 3)
    cos = jnp.concatenate([cosine()[...]] * 2, 1)
    sin = jnp.concatenate([sine()[...]] * 2, 1)
    joint = dot(first, w_joint()[...]) + params[4:5, : 3 * LOCAL]
    query = turn(joint[:, :LOCAL], cos, sin)
    keys = turn(joint[:, LOCAL : 2 * LOCAL], cos, sin).astype(LOW)
    values = joint[:, 2 * LOCAL :].astype(LOW)
    if keep:
        out[4][...] = query.astype(LOW)
        out[5][...] = keys
        out[6][...] = values
        store(4, 5, 6)
    contexts = []
    for seq in range(2):
        part = slice(seq * SEQ, seq * SEQ + SEQ)
        scores = by_head(dot_back(head_stack(query[part]), keys[part]))
        scores = jnp.where(
            allowed_keys(seg_row()[seq], seg_col()[seq])[None],
            scores * HEAD_DIM**-0.5,
            -1000000000.0,
        )
        top = jnp.max(scores, -1, keepdims=True)
        weight = jnp.exp(scores - top)
        total = jnp.sum(weight, -1, keepdims=True)
        probs = (weight * (1.0 / total)).astype(LOW).reshape(HERE * SEQ, SEQ)
        contexts.append(head_pick(by_head(dot(probs, values[part]))).astype(LOW))
        if keep:
            out[7][pl.ds(seq * HERE, HERE)] = top + jnp.log(total)
    context = jnp.concatenate(contexts, 0)
    if keep:
        out[8][...] = context
        store(7, 8)
    upward = dot(second, w_up()[...]) + params[5:6]
    half = 0.5 * (1.0 + lax.erf(upward * math.sqrt(0.5)))
    active = (upward * half).astype(LOW)
    if keep:
        out[9][...] = active
        slope = half + upward * jnp.exp(-0.5 * upward * upward) * math.sqrt(0.5 / math.pi)
        out[10][...] = slope.astype(LOW)
        store(9, 10)
    result = (dot(context, w_out()[:, :D]) + dot(active, w_down()[...])).astype(LOW)
    out[0][...] = result[:SEQ]
    out[1][...] = result[SEQ:]
    store(0, 1)


def backward_kernel(keep, load, out, store):
    (grad, w_out, seg_row, seg_col, query_in, keys_in, values_in, lse_in) = load[:8]
    (cosine, sine, params, w_joint, w_down, slope, w_up, hidden) = load[8:]
    g = grad()[...]
    context_grad = dot_back(g, w_out()[:, :D])
    turned = []
    for seq in range(2):
        part = slice(seq * SEQ, seq * SEQ + SEQ)
        query = query_in()[part]
        keys = keys_in()[part]
        values = values_in()[part]
        queries = head_stack(query)
        contexts = head_stack(context_grad[part])
        scores = by_head(dot_back(queries, keys))
        scores = jnp.where(
            allowed_keys(seg_row()[seq], seg_col()[seq])[None],
            scores * HEAD_DIM**-0.5,
            -1000000000.0,
        )
        probs = jnp.exp(scores - lse_in()[pl.ds(seq * HERE, HERE)])
        probs_grad = by_head(dot_back(contexts, values))
        scores_grad = probs * (probs_grad - jnp.sum(probs * probs_grad, -1, keepdims=True))
        scores_grad = scores_grad.astype(LOW).reshape(HERE * SEQ, SEQ)
        probs = probs.astype(LOW).reshape(HERE * SEQ, SEQ)
        query_grad = head_pick(by_head(dot(scores_grad, keys)))
        keys_grad = dot_over(scores_grad, queries)
        values_grad = dot_over(probs, contexts)
        cos = jnp.concatenate([cosine()[part]] * 2, 1)
        sin = -jnp.concatenate([sine()[part]] * 2, 1)
        turned.append(
            jnp.concatenate(
                [
                    turn(query_grad * HEAD_DIM**-0.5, cos, sin),
                    turn(keys_grad * HEAD_DIM**-0.5, cos, sin),
                    values_grad,
                ],
                1,
            ).astype(LOW)
        )
    joint_grad = jnp.concatenate(turned, 0)
    if keep:
        out[3][...] = joint_grad
        store(3)
    first_grad = dot_back(joint_grad, w_joint()[...])
    up_grad = dot_back(g, w_down()[...]) * slope()[...].astype(FULL)
    up_grad = up_grad.astype(LOW)
    if keep:
        out[2][...] = up_grad
        store(2)
    second_grad = dot_back(up_grad, w_up()[...])
    normed, scale = normalize(hidden()[...].astype(FULL))
    params = params()
    inner = first_grad * params[0:1] + second_grad * params[2:3]
    back = scale * (
        inner
        - jnp.mean(inner, -1, keepdims=True)
        - normed * jnp.mean(inner * normed, -1, keepdims=True)
    )
    result = back.astype(LOW)
    out[0][...] = result[:SEQ]
    out[1][...] = result[SEQ:]
    store(0, 1)
    if keep:
        out[4][...] = jnp.zeros(out[4].shape, FULL)
        for row, item in (
            (0, first_grad * normed),
            (1, first_grad),
            (2, second_grad * normed),
            (3, second_grad),
            (4, up_grad.astype(FULL)),
            (5, g.astype(FULL)),
            (6, joint_grad.astype(FULL)),
        ):
            out[4][row : row + 1, : item.shape[1]] = jnp.sum(item, 0, keepdims=True)
        store(4)


JOINT = slice(0, 3 * LOCAL)
UP = slice(3 * LOCAL, 3 * LOCAL + FEED)
DOWN = slice(3 * LOCAL + FEED, 3 * LOCAL + FEED + D)
TOKENS = 2 * SEQ


class Pieces:
    def __init__(self, refs):
        self.refs = refs

    def __getitem__(self, index):
        return jnp.concatenate([ref[...] for ref in self.refs], 0)[index]


def call(kernel, name, operands, shapes, flops):
    arrays = []

    def number(array):
        for place, item in enumerate(arrays):
            if item is array:
                return place
        arrays.append(array)
        return len(arrays) - 1

    views = []
    for operand in operands:
        if isinstance(operand[-1], slice):
            views.append((number(operand[0]), operand[1]))
        else:
            views.append([number(array) for array in operand])

    def body(*refs):
        sources, results = refs[: len(arrays)], refs[len(arrays) :]

        def loader(view):
            if isinstance(view, tuple):
                return lambda: sources[view[0]].at[:, view[1]]
            if len(view) == 1:
                return lambda: sources[view[0]]
            return lambda: Pieces([sources[place] for place in view])

        kernel([loader(view) for view in views], results, lambda *numbers: None)

    return pl.pallas_call(
        body,
        in_specs=[pl.BlockSpec(memory_space=pltpu.VMEM)] * len(arrays),
        out_specs=[pl.BlockSpec(memory_space=pltpu.VMEM)] * len(shapes),
        out_shape=[jax.ShapeDtypeStruct(shape, kind) for shape, kind in shapes],
        compiler_params=pltpu.CompilerParams(vmem_limit_bytes=16 * 1024 * 1024),
        cost_estimate=flops
        and pl.CostEstimate(flops=flops, bytes_accessed=8 * D * D, transcendentals=0),
        name=name,
    )(*arrays)


def own_call(kernel, name, operands, shapes, flops, early):
    arrays = []
    parts = []
    held = []
    for operand in operands:
        if isinstance(operand[-1], slice):
            array, columns = operand
            parts.append([(len(arrays), columns, None)])
            arrays.append(array)
            held.append(((array.shape[0], columns.stop - columns.start), array.dtype))
        else:
            row = 0
            pieces = []
            for array in operand:
                whole = None if len(operand) == 1 else pl.ds(row, array.shape[0])
                pieces.append((len(arrays), None, whole))
                arrays.append(array)
                row += array.shape[0]
            parts.append(pieces)
            held.append(((row,) + operand[0].shape[1:], operand[0].dtype))

    def body(*refs):
        sources, refs = refs[: len(arrays)], refs[len(arrays) :]
        results, refs = refs[: len(shapes)], refs[len(shapes) :]
        near, refs = refs[: len(held)], refs[len(held) :]
        kept, (come, go) = refs[: len(shapes)], refs[len(shapes) :]
        copies = []
        for pieces, ref in zip(parts, near):
            group = []
            for index, columns, place in pieces:
                source = sources[index] if columns is None else sources[index].at[:, columns]
                target = ref if place is None else ref.at[place]
                group.append(pltpu.make_async_copy(source, target, come.at[index]))
            copies.append(group)
        for group in copies[:early]:
            for copy in group:
                copy.start()
        done = set()

        def loader(number):
            def load():
                if number not in done:
                    done.add(number)
                    for copy in copies[number]:
                        copy.wait()
                return near[number]

            return load

        sent = []

        def store(*numbers):
            for number in numbers:
                copy = pltpu.make_async_copy(kept[number], results[number], go.at[number])
                copy.start()
                sent.append(copy)

        loaders = [loader(number) for number in range(len(held))]
        for load in loaders[:early]:
            load()
        for group in copies[early:]:
            for copy in group:
                copy.start()
        kernel(loaders, kept, store)
        for load in loaders:
            load()
        for copy in sent:
            copy.wait()

    return pl.pallas_call(
        body,
        in_specs=[pl.BlockSpec(memory_space=pltpu.HBM)] * len(arrays),
        out_specs=[pl.BlockSpec(memory_space=pltpu.HBM)] * len(shapes),
        out_shape=[jax.ShapeDtypeStruct(shape, kind) for shape, kind in shapes],
        scratch_shapes=[pltpu.VMEM(shape, kind) for shape, kind in held]
        + [pltpu.VMEM(shape, kind) for shape, kind in shapes]
        + [pltpu.SemaphoreType.DMA((len(arrays),)), pltpu.SemaphoreType.DMA((len(shapes),))],
        compiler_params=pltpu.CompilerParams(vmem_limit_bytes=VMEM),
        cost_estimate=flops
        and pl.CostEstimate(flops=flops, bytes_accessed=8 * D * D, transcendentals=0),
        name=name,
    )(*arrays)


ESTIMATE = TOKENS * 16 * D * D
HALVES = [((SEQ, D), LOW)] * 2


def forward(hidden, place, layer, keep):
    seg_row, seg_col, cosine, sine = ((item,) for item in place)
    params, weights, w_out = layer
    shapes = list(HALVES)
    if keep:
        wide = ((TOKENS, D), LOW)
        narrow = ((TOKENS, LOCAL), LOW)
        lse = ((2 * HERE, SEQ, 1), FULL)
        shapes += [wide, wide, narrow, narrow, narrow, lse, narrow, wide, wide]
    operands = (
        hidden,
        seg_row,
        seg_col,
        cosine,
        sine,
        (params,),
        (weights, JOINT),
        (w_out,),
        (weights, UP),
        (weights, DOWN),
    )
    kernel = functools.partial(forward_kernel, keep)
    return call(kernel, "layer_forward", operands, shapes, ESTIMATE)


def backward(grad, hidden, place, layer, saved, keep, alone=False):
    seg_row, seg_col, cosine, sine = ((item,) for item in place)
    params, weights, w_out = layer
    shapes = list(HALVES)
    if keep:
        shapes += [((TOKENS, FEED), LOW), ((TOKENS, 3 * LOCAL), LOW), ((8, D), FULL)]
    operands = (
        grad,
        (w_out,),
        seg_row,
        seg_col,
        *((item,) for item in saved[2:6]),
        cosine,
        sine,
        (params,),
        (weights, JOINT),
        (weights, DOWN),
        (saved[8],),
        (weights, UP),
        hidden,
    )
    kernel = functools.partial(backward_kernel, keep)
    if alone:
        return own_call(kernel, "layer_backward_alone", operands, shapes, ESTIMATE, 10)
    return call(kernel, "layer_backward", operands, shapes, ESTIMATE)


def lower_upper(lower, upper, half):
    lane = lax.broadcasted_iota(jnp.int32, lower.shape, 1)
    if half == 0:
        return jnp.where(lane < HEAD_DIM, lower, pltpu.roll(upper, HEAD_DIM, 1))
    return jnp.where(lane < HEAD_DIM, pltpu.roll(lower, HEAD_DIM, 1), upper)


def choose_kernel(place, joint, up, out):
    c, k = place[0], place[1]

    def group(ref, index):
        return ref[:, pl.ds(pl.multiple_of(index * 128, 128), 128)].astype(FULL)

    for pair_ in range(6):
        lower = group(joint, 4 * pair_ + c)
        upper = group(joint, 4 * pair_ + 2 + c)
        here = slice(pair_ * 128, pair_ * 128 + 128)
        out[k, :, here] = lower_upper(lower, upper, 0).astype(LOW)
        out[1 - k, :, here] = lower_upper(lower, upper, 1).astype(LOW)
    for pair_ in range(8):
        here = slice(3 * LOCAL + pair_ * 128, 3 * LOCAL + pair_ * 128 + 128)
        for slot, core in ((0, k), (1, 1 - k)):
            lower = group(up, 4 * pair_ + core)
            upper = group(up, 4 * pair_ + 2 + core)
            block = jnp.where(
                jnp.zeros(lower.shape, jnp.int32) + c == 0,
                lower_upper(lower, upper, 0),
                lower_upper(lower, upper, 1),
            )
            out[slot, :, here] = block.astype(LOW)


def finish_kernel(
    place, block, down_in, out_own, out_other, sums, joint, out, up, down, *rest
):
    vectors, (whole, up_all, joint_all) = rest[:8], rest[8:]

    def quarter(c, k, column):
        return block[c, 32 * k : 32 * k + 32, column : column + 128].astype(FULL)

    def vector(c, k, column):
        return sums[2 * c + k, :, column : column + 128]

    for p in range(16):
        at = p // 2 * 128
        for k in range(2):
            here = slice((2 * p + k) * 128, (2 * p + k) * 128 + 128)
            up[0, :, here] = lower_upper(quarter(0, k, at), quarter(1, k, at), p % 2)
            up_all[:, here] = lower_upper(vector(0, k, at), vector(1, k, at), p % 2)
    for t in range(12):
        at = t // 2 * 128
        for c in range(2):
            here = slice((2 * t + c) * 128, (2 * t + c) * 128 + 128)
            joint[0, :, here] = lower_upper(
                quarter(c, 0, FEED + at), quarter(c, 1, FEED + at), t % 2
            )
            joint_all[:, here] = lower_upper(vector(c, 0, at), vector(c, 1, at), t % 2)
    joint_all[:, 3 * D :] = jnp.zeros((8, 128), FULL)
    for c in range(2):
        down[0, 64 * c : 64 * c + 64] = down_in[c].astype(FULL)
    out[0] = out_own[...].astype(FULL) + out_other[...].astype(FULL)
    whole[...] = sums[0] + sums[1] + sums[2] + sums[3]
    whole[5:6] = sums[0, 5:6]
    f = place[0]

    def lanes(ref, start, width):
        first = pl.multiple_of(start // 128 * 128, 128)
        return pltpu.roll(ref[:, pl.ds(first, width)], (width - start % 128) % width, 1)

    shares = lanes(whole, f * 32, 128)
    for index, row in ((0, 0), (1, 1), (3, 5), (4, 2), (5, 3), (7, 5)):
        vectors[index][...] = shares[row : row + 1, :32]
    vectors[2][...] = lanes(joint_all, f * 96, 256)[6:7, :96]
    vectors[6][...] = up_all[4:5, pl.ds(pl.multiple_of(f * 128, 128), 128)]


def down_kernel(load, out, store):
    active, grad = load
    out[0][...] = dot_over(active()[...], grad()[...]).astype(LOW)
    store(0)


def weights_kernel(load, out, store):
    second, up_grad, context, grad, first, joint_grad = load
    one, two = out
    up = dot_over(second()[...], up_grad()[...]).astype(LOW)
    one[:, :SPLIT] = up[:, :SPLIT]
    two[:, : FEED - SPLIT] = up[:, SPLIT:]
    term = dot_over(context()[...], grad()[...]).astype(LOW)
    for y in range(4):
        for x in range(4):
            rows = slice((4 * y + x) * 64, (4 * y + x) * 64 + 64)
            one[rows, SPLIT:] = term[64 * y : 64 * y + 64, LOCAL * x : LOCAL * x + LOCAL]
    store(0)
    two[:, FEED - SPLIT :] = dot_over(first()[...], joint_grad()[...]).astype(LOW)
    store(1)


SPLIT = 768


def simple_call(kernel, name, operands, shapes, scalars=0, scratch=()):
    return pl.pallas_call(
        kernel,
        in_specs=[pl.BlockSpec(memory_space=pltpu.SMEM)] * scalars
        + [pl.BlockSpec(memory_space=pltpu.VMEM)] * (len(operands) - scalars),
        out_specs=[pl.BlockSpec(memory_space=pltpu.VMEM)] * len(shapes),
        out_shape=[jax.ShapeDtypeStruct(shape, kind) for shape, kind in shapes],
        scratch_shapes=[pltpu.VMEM(shape, FULL) for shape in scratch],
        compiler_params=pltpu.CompilerParams(vmem_limit_bytes=24 * 1024 * 1024),
        name=name,
    )(*operands)


SMALL = (32, 32, 96, 32, 32, 32, 128, 32)
EDGES = [sum(SMALL[:i]) for i in range(len(SMALL) + 1)]


def choose_columns(joint_weight, up_weight):
    c = lax.axis_index("ctx")
    k = lax.axis_index("core")
    (chosen,) = simple_call(
        choose_kernel,
        "choose_columns",
        (jnp.stack([c, k]), joint_weight, up_weight),
        [((2, 32, 3 * LOCAL + FEED), LOW)],
        1,
    )
    return in_order(k, chosen[0], shift(chosen[1], "core", 1), 0)


def fetch_layer(block, tokens, small, output_weight, down_weight):
    c = lax.axis_index("ctx")
    k = lax.axis_index("core")
    quarter = 2 * c + k
    down = lax.dynamic_slice_in_dim(down_weight, c * 64, 64, 0)
    block = jnp.concatenate([block, down], 1)
    weights = lax.all_gather(block, ("y", "x"), axis=0, tiled=True)
    vectors = jnp.concatenate(small + (jnp.zeros((512 - sum(SMALL),), LOW),)).reshape(4, 128)
    vectors = jnp.concatenate([vectors, jnp.zeros((28, 128), LOW)], 0)
    mixed = pair(after(jnp.concatenate([output_weight, vectors], 1), block), "core", 0)
    others, (got,) = together(direct_blocks(mixed, "x"), [shift(tokens[0], "ctx", 1)])
    later, got = lax.optimization_barrier((tokens[1], got))
    inputs = in_order(c, tokens[0], got, 1)
    mixed = stack_four(mixed, others, "x")
    out = lax.dynamic_index_in_dim(mixed, quarter, 0, False)[:, :D]
    vectors = mixed[:, :, D:].reshape(4, 2, 32, 128)[:, :, :8].reshape(64, 128)
    out = jnp.concatenate([out, vectors], 1)
    others, (inputs_other, got) = together(
        direct_blocks(out, "y"), [shift(inputs, "core", 1), shift(later, "ctx", 1)]
    )
    cotangent = in_order(c, later, got, 1)
    out = stack_four(out, others, "y")
    inputs = (inputs, inputs_other)
    cotangent = (cotangent, shift(cotangent, "core", 1))
    vectors = out[:, :, D:].reshape(32, 8, 128)[:, :4].reshape(32, 512)
    small = [vectors[:, a:b].reshape(-1).astype(FULL) for a, b in zip(EDGES, EDGES[1:])]
    joint_bias = lax.dynamic_index_in_dim(
        small[2].reshape(3, 4, 4, HEAD_DIM), quarter, 2, False
    ).reshape(-1)
    up_bias = small[6].reshape(16, 2, 2, HEAD_DIM)
    up_bias = lax.dynamic_index_in_dim(
        lax.dynamic_index_in_dim(up_bias, c, 2, False), k, 1, False
    ).reshape(-1)
    params = jnp.stack(
        [
            small[0],
            small[1],
            small[4],
            small[5],
            jnp.pad(joint_bias, (0, D - 3 * LOCAL)),
            up_bias,
            small[3] + small[7],
            jnp.zeros((D,), FULL),
        ]
    )
    layer = (params, weights, out.reshape(LOCAL, D + 128))
    return layer, inputs, cotangent


def return_layer(one, two, down, sums, beside, late):
    c = lax.axis_index("ctx")
    k = lax.axis_index("core")
    x = lax.axis_index("x")
    y = lax.axis_index("y")
    one = one.reshape(4, 4, 64, -1)
    two = two.reshape(4, 4, 64, -1)
    sums = sums + shift_pair(sums, "y", 1)
    ones, twos, (more, beside, core) = together(
        ring_start(one, "y", 0),
        ring_start(two, "x", 1),
        [shift_pair(sums, "y", 2), beside, late[1]],
    )
    sums = sums + more
    own, give = halves_of(late[0], core)
    ones, twos, (more, got) = together(
        ring_next(one, "y", 0, *ones),
        ring_next(two, "x", 1, *twos),
        [shift_pair(sums, "x", 1), shift(give, "ctx", 1)],
    )
    sums = sums + more
    one = plus(quarter_of(one, 0, y), *ones)
    two = plus(quarter_of(two, 1, x), *twos)
    out = one[:, :, SPLIT :].transpose(1, 0, 2).reshape(1, 64, D)
    out = jnp.where(
        jnp.arange(4)[:, None, None] == 2 * c + k, out, jnp.zeros_like(out)
    )
    one = jnp.concatenate([one[:, :, : SPLIT], out], -1)
    ones, twos, (more, down_more) = together(
        direct(one, "x", 0),
        direct(two, "y", 0),
        [shift_pair(sums, "x", 2), shift(down, "ctx", 1)],
    )
    sums = sums + more
    one = plus(quarter_of(one, 0, x), *ones)
    two = plus(quarter_of(two, 0, y), *twos)
    both = jnp.concatenate([one[:, :SPLIT], two, one[:, SPLIT:]], 1)
    both = both.reshape(2, 32, -1)
    width = FEED + 3 * LOCAL
    mine = take(both, k, 0)
    (other,), (more,) = together(
        [shift(take(both, 1 - k, 0), "core", 1)], [shift(sums, "core", 1)]
    )
    sums = in_order(k, sums[None], more[None], 0)
    block = in_order(k, mine[:, :width], other[:, :width], 0)
    out = plus(mine[:, width:], other[:, width:])
    (block_more, out_more, sums_more), _ = together(
        [shift(block, "ctx", 1), shift(out, "ctx", 1), shift(sums, "ctx", 1)], [beside]
    )
    place = (4 * y + x) * 2 + k
    vectors = [((1, width), FULL) for width in SMALL]
    joint, out, up, down, *vectors = simple_call(
        finish_kernel,
        "finish",
        (
            place[None],
            in_order(c, block[None], block_more[None], 0),
            in_order(c, down[None], down_more[None], 0),
            out,
            out_more,
            in_order(c, sums, sums_more, 0),
        ),
        [((1, 32, 3 * D), FULL), ((1, 32, D), FULL), ((1, 32, 4 * D), FULL), ((1, 128, D), FULL)]
        + vectors,
        1,
        ((8, D), (8, 4 * D), (8, 3 * D + 128)),
    )
    return joint, out, up, down, vectors, beside, own + got.astype(FULL)


def plus_full(left, right):
    return left.astype(FULL) + right.astype(FULL)


def take(block, index, dim):
    return lax.dynamic_index_in_dim(block, index, dim, False)


def halves_of(mine, other):
    c = lax.axis_index("ctx")
    total = plus_full(mine, other)
    total = total.reshape(total.shape[:-2] + (2, SEQ // 2, D))
    dim = total.ndim - 3
    return take(total, c, dim), take(total, 1 - c, dim).astype(LOW)


def sum_cores(mine, other):
    return halves_of(mine, shift(other, "core", 1))


def send_on(block):
    same = lax.ppermute(block, ("section", "ctx"), [(i, (i + 2) % 4) for i in range(4)])
    flip = lax.ppermute(block, ("section", "ctx"), [(i, 3 - i) for i in range(4)])
    return same, flip


def join(keep, whole, same, flip):
    mine = jnp.where(keep, whole, in_order(lax.axis_index("ctx"), same, flip, 0))
    return mine, shift(mine, "core", 1)


def split_two(results):
    return results[0], results[1], results[2:]


def shards(
    inputs,
    cotangent,
    segments,
    positions,
    attention_gain,
    attention_bias,
    joint_weight,
    joint_bias,
    output_weight,
    output_bias,
    feed_gain,
    feed_bias,
    up_weight,
    up_bias,
    down_weight,
    down_bias,
):
    section = lax.axis_index("section")
    count = inputs.shape[0]
    block = choose_columns(joint_weight[0], up_weight[0])
    pos = pair(after(positions[:, 0], block), "ctx", 1)
    pos = jnp.stack([pos, shift(pos, "core", 1)], 1)
    seg = after(segments[:, 0], block)
    seg = jnp.stack([seg, shift(seg, "core", 1)], 1)
    early, pos, seg = lax.optimization_barrier((inputs[:, 0], pos, seg))
    layer, whole_in, whole_grad = fetch_layer(
        block,
        (early, cotangent[:, 0]),
        (
            attention_gain[0],
            attention_bias[0],
            joint_bias[0],
            output_bias[0],
            feed_gain[0],
            feed_bias[0],
            up_bias[0],
            down_bias[0],
        ),
        output_weight[0],
        down_weight[0],
    )
    bias = layer[0][6]
    lane = jnp.arange(128) % HEAD_DIM
    rates = jnp.where(lane < ROT, 10000.0 ** (-2.0 * (lane % (ROT // 2)).astype(FULL) / ROT), 0.0)
    angle = pos.astype(FULL)[..., None] * rates
    cosine = jnp.cos(angle).reshape(count, TOKENS, 128)
    sine = (jnp.sin(angle) * jnp.where(lane < ROT // 2, -1.0, 1.0)).reshape(count, TOKENS, 128)
    places = [(seg[m][:, None, :], seg[m][:, :, None], cosine[m], sine[m]) for m in range(count)]
    c = lax.axis_index("ctx")

    def of(pair_, m):
        return tuple(item[m] for item in pair_)

    def own_tokens(whole):
        return take(whole.reshape(2, SEQ // 2, D), c, 0).astype(FULL)

    def over_ctx(base, own, give):
        return (base + own + shift(give, "ctx", 1).astype(FULL)).astype(LOW)

    own_in = inputs[:, 0].astype(FULL) + bias
    part = forward(of(whole_in, 0), places[0], layer, False)
    own, give = sum_cores(*part)
    a, b = of(whole_in, 1)
    part = forward((after(a, give), b), places[1], layer, False)
    result = over_ctx(own_in[0], own, give)
    sent = [send_on(result)]
    own, give = sum_cores(part[0], after(part[1], result))
    result = over_ctx(own_in[1], own, give)
    sent.append(send_on(result))
    own_grad = cotangent[:, 0].astype(FULL)
    same, flip, _ = lax.optimization_barrier((*sent[0], result))
    hidden = [join(section == 0, whole_in[0][0], same, flip)]
    *out_zero, saved_zero = split_two(forward(hidden[0], places[0], layer, True))
    part = backward(of(whole_grad, 0), hidden[0], places[0], layer, saved_zero, False)
    own, give = sum_cores(*part)
    same, flip, _ = lax.optimization_barrier((*sent[1], part[0]))
    a, b = join(section == 0, whole_in[0][1], same, flip)
    hidden.append((a, after(b, give)))
    *out_one, saved_one = split_two(forward(hidden[1], places[1], layer, True))
    got = after(shift(give, "ctx", 1), out_one[0])
    result = (own_grad[0] + own + got.astype(FULL)).astype(LOW)
    sent = [send_on(result)]
    a, b = of(whole_grad, 1)
    part = backward((after(a, result), b), hidden[1], places[1], layer, saved_one, False)
    same, flip, *part = lax.optimization_barrier((*sent[0], *part))
    a, b = join(section == 1, whole_grad[0][0], same, flip)
    own, give = sum_cores(*part)
    result = over_ctx(own_grad[1], own, give)
    sent.append(send_on(result))
    saved = [saved_zero, saved_one]
    grads = [(a, after(b, result))]

    def last(m):
        return backward(grads[m], hidden[m], places[m], layer, saved[m], True, m == 1)

    *part_zero, up_zero, joint_zero, sums_zero = last(0)
    same, flip, part_zero[0] = lax.optimization_barrier((*sent[1], part_zero[0]))
    grads.append(join(section == 1, whole_grad[0][1], same, flip))
    both = (*grads[0], *grads[1])
    (down,) = call(
        down_kernel,
        "down_gradient",
        ((saved_zero[7], saved_one[7]), both),
        [((FEED, D), LOW)],
        None,
    )
    down_share = lax.psum_scatter(down, ("y", "x"), scatter_dimension=0, tiled=True)
    ready = grads[1][1]
    outs = [
        jnp.stack([out_zero[i], out_one[i], after(part_zero[i], ready)]) for i in range(2)
    ]
    grads[1] = (grads[1][0], after(grads[1][1], down))
    *part_one, up_one, joint_one, sums_one = last(1)
    own_early, give = sum_cores(*outs)
    one, two = own_call(
        weights_kernel,
        "weight_gradients",
        (
            (saved_zero[1], saved_one[1]),
            (up_zero, up_one),
            (saved_zero[6], saved_one[6]),
            (after(both[0], give), *both[1:]),
            (saved_zero[0], saved_one[0]),
            (joint_zero, joint_one),
        ),
        [((D, SPLIT + LOCAL), LOW), ((D, FEED - SPLIT + 3 * LOCAL), LOW)],
        None,
        2,
    )
    joint_grad, out_grad, up_grad, down_grad, small, got, late = return_layer(
        one,
        two,
        down_share,
        sums_zero + sums_one,
        shift(give, "ctx", 1),
        (part_one[0], shift(part_one[1], "core", 1)),
    )
    base = jnp.stack(
        [own_tokens(hidden[0][0]) + bias, own_tokens(hidden[1][0]) + bias, own_tokens(grads[0][0])]
    )
    early = (base + own_early + got.astype(FULL)).astype(LOW)
    late = (own_tokens(grads[1][0])[None] + late).astype(LOW)
    section_out = early[None, :2, None]
    input_grad = jnp.concatenate([early[2:], late])[None, :, None]
    return (
        section_out,
        input_grad,
        small[0],
        small[1],
        joint_grad,
        small[2],
        out_grad,
        small[3],
        small[4],
        small[5],
        up_grad,
        small[6],
        down_grad,
        small[7],
    )


def solution(mesh):
    finer = Mesh(mesh.devices.reshape(2, 2, 4, 4, 2), ("section", "ctx", "y", "x", "core"))
    fsdp = ("y", "x", "core")
    vector = P("section", fsdp)
    matrix = P("section", fsdp, None)
    tokens = P(None, fsdp, "ctx", None)
    kept = P("section", None, fsdp, "ctx", None)
    params = (
        vector,
        vector,
        matrix,
        vector,
        matrix,
        vector,
        vector,
        vector,
        matrix,
        vector,
        matrix,
        vector,
    )
    return jax.shard_map(
        shards,
        mesh=finer,
        in_specs=(tokens, tokens, P(None, fsdp, None), P(None, fsdp, "ctx")) + params,
        out_specs=(kept, kept) + params,
        check_vma=False,
    )
```

```python
import functools
import math

import jax
import jax.numpy as jnp
from jax import lax
from jax.experimental import pallas as pl
from jax.experimental.pallas import tpu as pltpu
from jax.sharding import Mesh
from jax.sharding import PartitionSpec as P

D = 1024
HEAD_DIM = 64
ROT = 16
SEQ = 256
LOCAL = 256
FEED = 1024
HERE = LOCAL // HEAD_DIM
EPSILON = 1e-05
LOW = jnp.bfloat16
FULL = jnp.float32
VMEM = 60 * 1024 * 1024


def shift(block, axis, distance):
    size = lax.axis_size(axis)
    return lax.ppermute(block, axis, [(i, (i + distance) % size) for i in range(size)])


def direct_blocks(block, axis):
    return [shift(block, axis, d) for d in (1, 2, 3)]


def stack_four(block, others, axis):
    me = lax.axis_index(axis)
    whole = jnp.zeros((4,) + block.shape, block.dtype)
    for distance, part in enumerate((block, *others)):
        whole = lax.dynamic_update_slice_in_dim(whole, part[None], (me - distance) % 4, 0)
    return whole


def shift_pair(block, axis, apart):
    size = lax.axis_size(axis)
    return lax.ppermute(block, axis, [(i, i ^ apart) for i in range(size)])


def quarter_of(block, dim, index):
    return lax.dynamic_index_in_dim(block, index % 4, dim, False)


def ring_start(block, axis, dim):
    far = quarter_of(block, dim, lax.axis_index(axis) + 2)
    cut = far.shape[-1] // 2
    return [shift(far[..., :cut], axis, 1), shift(far[..., cut:], axis, -1)]


def ring_next(block, axis, dim, up, down):
    me = lax.axis_index(axis)
    cut = up.shape[-1]
    ahead = quarter_of(block, dim, me + 1)
    behind = quarter_of(block, dim, me - 1)
    ahead = jnp.concatenate([plus(ahead[..., :cut], up), ahead[..., cut:]], -1)
    behind = jnp.concatenate([behind[..., :cut], plus(behind[..., cut:], down)], -1)
    return [shift(ahead, axis, 1), shift(behind, axis, -1)]


def direct(block, axis, dim):
    me = lax.axis_index(axis)
    return [shift(quarter_of(block, dim, me + d), axis, d) for d in (1, 3, 2)]


def together(*groups):
    flat = lax.optimization_barrier(tuple(item for group in groups for item in group))
    result = []
    for group in groups:
        result.append(flat[: len(group)])
        flat = flat[len(group) :]
    return result


def plus(*terms):
    return sum(term.astype(FULL) for term in terms).astype(LOW)


def after(block, *others):
    return lax.optimization_barrier((block,) + others)[0]


def in_order(index, own, other, dim):
    return jnp.where(
        index == 0,
        jnp.concatenate([own, other], dim),
        jnp.concatenate([other, own], dim),
    )


def pair(block, axis, dim):
    return in_order(lax.axis_index(axis), block, shift(block, axis, 1), dim)


def dot(left, right):
    return jnp.dot(left, right, preferred_element_type=FULL)


def dot_back(left, right):
    return lax.dot_general(left, right, (((1,), (1,)), ((), ())), preferred_element_type=FULL)


def dot_over(left, right):
    return lax.dot_general(left, right, (((0,), (0,)), ((), ())), preferred_element_type=FULL)


def turn(heads, cosine, sine):
    lane = lax.broadcasted_iota(jnp.int32, heads.shape, 1) % HEAD_DIM
    partner = jnp.where(
        lane < ROT // 2,
        pltpu.roll(heads, LOCAL - ROT // 2, 1),
        pltpu.roll(heads, ROT // 2, 1),
    )
    return heads * cosine + partner * sine


def normalize(hidden):
    centred = hidden - jnp.mean(hidden, -1, keepdims=True)
    scale = lax.rsqrt(jnp.mean(centred * centred, -1, keepdims=True) + EPSILON)
    return centred * scale, scale


def head_lanes(head):
    lane = lax.broadcasted_iota(jnp.int32, (SEQ, LOCAL), 1)
    return lane // HEAD_DIM == head


def head_stack(block):
    full = block.astype(FULL)
    copies = [jnp.where(head_lanes(head), full, 0.0) for head in range(HERE)]
    return jnp.concatenate(copies, 0).astype(LOW)


def head_pick(block):
    result = block[0]
    for head in range(1, HERE):
        result = jnp.where(head_lanes(head), block[head], result)
    return result


def by_head(block):
    return block.reshape(HERE, SEQ, SEQ)


def allowed_keys(seg_row, seg_col):
    query = lax.broadcasted_iota(jnp.int32, (SEQ, SEQ), 0)
    key = lax.broadcasted_iota(jnp.int32, (SEQ, SEQ), 1)
    return (seg_col == seg_row) & (query >= key)


def forward_kernel(keep, load, out, store):
    hidden, seg_row, seg_col, cosine, sine, params, w_joint, w_out, w_up, w_down = load
    normed, _ = normalize(hidden()[...].astype(FULL))
    params = params()
    first = (normed * params[0:1] + params[1:2]).astype(LOW)
    second = (normed * params[2:3] + params[3:4]).astype(LOW)
    if keep:
        out[2][...] = first
        out[3][...] = second
        store(2, 3)
    cos = jnp.concatenate([cosine()[...]] * 2, 1)
    sin = jnp.concatenate([sine()[...]] * 2, 1)
    joint = dot(first, w_joint()[...]) + params[4:5, : 3 * LOCAL]
    query = turn(joint[:, :LOCAL], cos, sin)
    keys = turn(joint[:, LOCAL : 2 * LOCAL], cos, sin).astype(LOW)
    values = joint[:, 2 * LOCAL :].astype(LOW)
    if keep:
        out[4][...] = query.astype(LOW)
        out[5][...] = keys
        out[6][...] = values
        store(4, 5, 6)
    contexts = []
    for seq in range(2):
        part = slice(seq * SEQ, seq * SEQ + SEQ)
        scores = by_head(dot_back(head_stack(query[part]), keys[part]))
        scores = jnp.where(
            allowed_keys(seg_row()[seq], seg_col()[seq])[None],
            scores * HEAD_DIM**-0.5,
            -1000000000.0,
        )
        top = jnp.max(scores, -1, keepdims=True)
        weight = jnp.exp(scores - top)
        total = jnp.sum(weight, -1, keepdims=True)
        probs = (weight * (1.0 / total)).astype(LOW).reshape(HERE * SEQ, SEQ)
        contexts.append(head_pick(by_head(dot(probs, values[part]))).astype(LOW))
        if keep:
            out[7][pl.ds(seq * HERE, HERE)] = top + jnp.log(total)
    context = jnp.concatenate(contexts, 0)
    if keep:
        out[8][...] = context
        store(7, 8)
    upward = dot(second, w_up()[...]) + params[5:6]
    half = 0.5 * (1.0 + lax.erf(upward * math.sqrt(0.5)))
    active = (upward * half).astype(LOW)
    if keep:
        out[9][...] = active
        slope = half + upward * jnp.exp(-0.5 * upward * upward) * math.sqrt(0.5 / math.pi)
        out[10][...] = slope.astype(LOW)
        store(9, 10)
    result = (dot(context, w_out()[:, :D]) + dot(active, w_down()[...])).astype(LOW)
    out[0][...] = result[:SEQ]
    out[1][...] = result[SEQ:]
    store(0, 1)


def backward_kernel(keep, load, out, store):
    (grad, w_out, seg_row, seg_col, query_in, keys_in, values_in, lse_in) = load[:8]
    (cosine, sine, params, w_joint, w_down, slope, w_up, hidden) = load[8:]
    g = grad()[...]
    context_grad = dot_back(g, w_out()[:, :D])
    turned = []
    for seq in range(2):
        part = slice(seq * SEQ, seq * SEQ + SEQ)
        query = query_in()[part]
        keys = keys_in()[part]
        values = values_in()[part]
        queries = head_stack(query)
        contexts = head_stack(context_grad[part])
        scores = by_head(dot_back(queries, keys))
        scores = jnp.where(
            allowed_keys(seg_row()[seq], seg_col()[seq])[None],
            scores * HEAD_DIM**-0.5,
            -1000000000.0,
        )
        probs = jnp.exp(scores - lse_in()[pl.ds(seq * HERE, HERE)])
        probs_grad = by_head(dot_back(contexts, values))
        scores_grad = probs * (probs_grad - jnp.sum(probs * probs_grad, -1, keepdims=True))
        scores_grad = scores_grad.astype(LOW).reshape(HERE * SEQ, SEQ)
        probs = probs.astype(LOW).reshape(HERE * SEQ, SEQ)
        query_grad = head_pick(by_head(dot(scores_grad, keys)))
        keys_grad = dot_over(scores_grad, queries)
        values_grad = dot_over(probs, contexts)
        cos = jnp.concatenate([cosine()[part]] * 2, 1)
        sin = -jnp.concatenate([sine()[part]] * 2, 1)
        turned.append(
            jnp.concatenate(
                [
                    turn(query_grad * HEAD_DIM**-0.5, cos, sin),
                    turn(keys_grad * HEAD_DIM**-0.5, cos, sin),
                    values_grad,
                ],
                1,
            ).astype(LOW)
        )
    joint_grad = jnp.concatenate(turned, 0)
    if keep:
        out[3][...] = joint_grad
        store(3)
    first_grad = dot_back(joint_grad, w_joint()[...])
    up_grad = dot_back(g, w_down()[...]) * slope()[...].astype(FULL)
    up_grad = up_grad.astype(LOW)
    if keep:
        out[2][...] = up_grad
        store(2)
    second_grad = dot_back(up_grad, w_up()[...])
    normed, scale = normalize(hidden()[...].astype(FULL))
    params = params()
    inner = first_grad * params[0:1] + second_grad * params[2:3]
    back = scale * (
        inner
        - jnp.mean(inner, -1, keepdims=True)
        - normed * jnp.mean(inner * normed, -1, keepdims=True)
    )
    result = back.astype(LOW)
    out[0][...] = result[:SEQ]
    out[1][...] = result[SEQ:]
    store(0, 1)
    if keep:
        out[4][...] = jnp.zeros(out[4].shape, FULL)
        for row, item in (
            (0, first_grad * normed),
            (1, first_grad),
            (2, second_grad * normed),
            (3, second_grad),
            (4, up_grad.astype(FULL)),
            (5, g.astype(FULL)),
            (6, joint_grad.astype(FULL)),
        ):
            out[4][row : row + 1, : item.shape[1]] = jnp.sum(item, 0, keepdims=True)
        store(4)


JOINT = slice(0, 3 * LOCAL)
UP = slice(3 * LOCAL, 3 * LOCAL + FEED)
DOWN = slice(3 * LOCAL + FEED, 3 * LOCAL + FEED + D)
TOKENS = 2 * SEQ


class Pieces:
    def __init__(self, refs):
        self.refs = refs

    def __getitem__(self, index):
        return jnp.concatenate([ref[...] for ref in self.refs], 0)[index]


def call(kernel, name, operands, shapes, flops):
    arrays = []

    def number(array):
        for place, item in enumerate(arrays):
            if item is array:
                return place
        arrays.append(array)
        return len(arrays) - 1

    views = []
    for operand in operands:
        if isinstance(operand[-1], slice):
            views.append((number(operand[0]), operand[1]))
        else:
            views.append([number(array) for array in operand])

    def body(*refs):
        sources, results = refs[: len(arrays)], refs[len(arrays) :]

        def loader(view):
            if isinstance(view, tuple):
                return lambda: sources[view[0]].at[:, view[1]]
            if len(view) == 1:
                return lambda: sources[view[0]]
            return lambda: Pieces([sources[place] for place in view])

        kernel([loader(view) for view in views], results, lambda *numbers: None)

    return pl.pallas_call(
        body,
        in_specs=[pl.BlockSpec(memory_space=pltpu.VMEM)] * len(arrays),
        out_specs=[pl.BlockSpec(memory_space=pltpu.VMEM)] * len(shapes),
        out_shape=[jax.ShapeDtypeStruct(shape, kind) for shape, kind in shapes],
        compiler_params=pltpu.CompilerParams(vmem_limit_bytes=16 * 1024 * 1024),
        cost_estimate=flops
        and pl.CostEstimate(flops=flops, bytes_accessed=8 * D * D, transcendentals=0),
        name=name,
    )(*arrays)


def own_call(kernel, name, operands, shapes, flops, early):
    arrays = []
    parts = []
    held = []
    for operand in operands:
        if isinstance(operand[-1], slice):
            array, columns = operand
            parts.append([(len(arrays), columns, None)])
            arrays.append(array)
            held.append(((array.shape[0], columns.stop - columns.start), array.dtype))
        else:
            row = 0
            pieces = []
            for array in operand:
                whole = None if len(operand) == 1 else pl.ds(row, array.shape[0])
                pieces.append((len(arrays), None, whole))
                arrays.append(array)
                row += array.shape[0]
            parts.append(pieces)
            held.append(((row,) + operand[0].shape[1:], operand[0].dtype))

    def body(*refs):
        sources, refs = refs[: len(arrays)], refs[len(arrays) :]
        results, refs = refs[: len(shapes)], refs[len(shapes) :]
        near, refs = refs[: len(held)], refs[len(held) :]
        kept, (come, go) = refs[: len(shapes)], refs[len(shapes) :]
        copies = []
        for pieces, ref in zip(parts, near):
            group = []
            for index, columns, place in pieces:
                source = sources[index] if columns is None else sources[index].at[:, columns]
                target = ref if place is None else ref.at[place]
                group.append(pltpu.make_async_copy(source, target, come.at[index]))
            copies.append(group)
        for group in copies[:early]:
            for copy in group:
                copy.start()
        done = set()

        def loader(number):
            def load():
                if number not in done:
                    done.add(number)
                    for copy in copies[number]:
                        copy.wait()
                return near[number]

            return load

        sent = []

        def store(*numbers):
            for number in numbers:
                copy = pltpu.make_async_copy(kept[number], results[number], go.at[number])
                copy.start()
                sent.append(copy)

        loaders = [loader(number) for number in range(len(held))]
        for load in loaders[:early]:
            load()
        for group in copies[early:]:
            for copy in group:
                copy.start()
        kernel(loaders, kept, store)
        for load in loaders:
            load()
        for copy in sent:
            copy.wait()

    return pl.pallas_call(
        body,
        in_specs=[pl.BlockSpec(memory_space=pltpu.HBM)] * len(arrays),
        out_specs=[pl.BlockSpec(memory_space=pltpu.HBM)] * len(shapes),
        out_shape=[jax.ShapeDtypeStruct(shape, kind) for shape, kind in shapes],
        scratch_shapes=[pltpu.VMEM(shape, kind) for shape, kind in held]
        + [pltpu.VMEM(shape, kind) for shape, kind in shapes]
        + [pltpu.SemaphoreType.DMA((len(arrays),)), pltpu.SemaphoreType.DMA((len(shapes),))],
        compiler_params=pltpu.CompilerParams(vmem_limit_bytes=VMEM),
        cost_estimate=flops
        and pl.CostEstimate(flops=flops, bytes_accessed=8 * D * D, transcendentals=0),
        name=name,
    )(*arrays)


ESTIMATE = TOKENS * 16 * D * D
HALVES = [((SEQ, D), LOW)] * 2


def forward(hidden, place, layer, keep):
    seg_row, seg_col, cosine, sine = ((item,) for item in place)
    params, weights, w_out = layer
    shapes = list(HALVES)
    if keep:
        wide = ((TOKENS, D), LOW)
        narrow = ((TOKENS, LOCAL), LOW)
        lse = ((2 * HERE, SEQ, 1), FULL)
        shapes += [wide, wide, narrow, narrow, narrow, lse, narrow, wide, wide]
    operands = (
        hidden,
        seg_row,
        seg_col,
        cosine,
        sine,
        (params,),
        (weights, JOINT),
        (w_out,),
        (weights, UP),
        (weights, DOWN),
    )
    kernel = functools.partial(forward_kernel, keep)
    return call(kernel, "layer_forward", operands, shapes, ESTIMATE)


def backward(grad, hidden, place, layer, saved, keep, alone=False):
    seg_row, seg_col, cosine, sine = ((item,) for item in place)
    params, weights, w_out = layer
    shapes = list(HALVES)
    if keep:
        shapes += [((TOKENS, FEED), LOW), ((TOKENS, 3 * LOCAL), LOW), ((8, D), FULL)]
    operands = (
        grad,
        (w_out,),
        seg_row,
        seg_col,
        *((item,) for item in saved[2:6]),
        cosine,
        sine,
        (params,),
        (weights, JOINT),
        (weights, DOWN),
        (saved[8],),
        (weights, UP),
        hidden,
    )
    kernel = functools.partial(backward_kernel, keep)
    if alone:
        return own_call(kernel, "layer_backward_alone", operands, shapes, ESTIMATE, 10)
    return call(kernel, "layer_backward", operands, shapes, ESTIMATE)


def lower_upper(lower, upper, half):
    lane = lax.broadcasted_iota(jnp.int32, lower.shape, 1)
    if half == 0:
        return jnp.where(lane < HEAD_DIM, lower, pltpu.roll(upper, HEAD_DIM, 1))
    return jnp.where(lane < HEAD_DIM, pltpu.roll(lower, HEAD_DIM, 1), upper)


def choose_kernel(place, joint, up, out):
    c, k = place[0], place[1]

    def group(ref, index):
        return ref[:, pl.ds(pl.multiple_of(index * 128, 128), 128)].astype(FULL)

    for pair_ in range(6):
        lower = group(joint, 4 * pair_ + c)
        upper = group(joint, 4 * pair_ + 2 + c)
        here = slice(pair_ * 128, pair_ * 128 + 128)
        out[k, :, here] = lower_upper(lower, upper, 0).astype(LOW)
        out[1 - k, :, here] = lower_upper(lower, upper, 1).astype(LOW)
    for pair_ in range(8):
        here = slice(3 * LOCAL + pair_ * 128, 3 * LOCAL + pair_ * 128 + 128)
        for slot, core in ((0, k), (1, 1 - k)):
            lower = group(up, 4 * pair_ + core)
            upper = group(up, 4 * pair_ + 2 + core)
            block = jnp.where(
                jnp.zeros(lower.shape, jnp.int32) + c == 0,
                lower_upper(lower, upper, 0),
                lower_upper(lower, upper, 1),
            )
            out[slot, :, here] = block.astype(LOW)


def finish_kernel(
    place, block, down_in, out_own, out_other, sums, joint, out, up, down, *rest
):
    vectors, (whole, up_all, joint_all) = rest[:8], rest[8:]

    def quarter(c, k, column):
        return block[c, 32 * k : 32 * k + 32, column : column + 128].astype(FULL)

    def vector(c, k, column):
        return sums[2 * c + k, :, column : column + 128]

    for p in range(16):
        at = p // 2 * 128
        for k in range(2):
            here = slice((2 * p + k) * 128, (2 * p + k) * 128 + 128)
            up[0, :, here] = lower_upper(quarter(0, k, at), quarter(1, k, at), p % 2)
            up_all[:, here] = lower_upper(vector(0, k, at), vector(1, k, at), p % 2)
    for t in range(12):
        at = t // 2 * 128
        for c in range(2):
            here = slice((2 * t + c) * 128, (2 * t + c) * 128 + 128)
            joint[0, :, here] = lower_upper(
                quarter(c, 0, FEED + at), quarter(c, 1, FEED + at), t % 2
            )
            joint_all[:, here] = lower_upper(vector(c, 0, at), vector(c, 1, at), t % 2)
    joint_all[:, 3 * D :] = jnp.zeros((8, 128), FULL)
    for c in range(2):
        down[0, 64 * c : 64 * c + 64] = down_in[c].astype(FULL)
    out[0] = out_own[...].astype(FULL) + out_other[...].astype(FULL)
    whole[...] = sums[0] + sums[1] + sums[2] + sums[3]
    whole[5:6] = sums[0, 5:6]
    f = place[0]

    def lanes(ref, start, width):
        first = pl.multiple_of(start // 128 * 128, 128)
        return pltpu.roll(ref[:, pl.ds(first, width)], (width - start % 128) % width, 1)

    shares = lanes(whole, f * 32, 128)
    for index, row in ((0, 0), (1, 1), (3, 5), (4, 2), (5, 3), (7, 5)):
        vectors[index][...] = shares[row : row + 1, :32]
    vectors[2][...] = lanes(joint_all, f * 96, 256)[6:7, :96]
    vectors[6][...] = up_all[4:5, pl.ds(pl.multiple_of(f * 128, 128), 128)]


def down_kernel(load, out, store):
    active, grad = load
    out[0][...] = dot_over(active()[...], grad()[...]).astype(LOW)
    store(0)


def weights_kernel(load, out, store):
    second, up_grad, context, grad, first, joint_grad = load
    one, two = out
    up = dot_over(second()[...], up_grad()[...]).astype(LOW)
    one[:, :SPLIT] = up[:, :SPLIT]
    two[:, : FEED - SPLIT] = up[:, SPLIT:]
    term = dot_over(context()[...], grad()[...]).astype(LOW)
    for y in range(4):
        for x in range(4):
            rows = slice((4 * y + x) * 64, (4 * y + x) * 64 + 64)
            one[rows, SPLIT:] = term[64 * y : 64 * y + 64, LOCAL * x : LOCAL * x + LOCAL]
    store(0)
    two[:, FEED - SPLIT :] = dot_over(first()[...], joint_grad()[...]).astype(LOW)
    store(1)


SPLIT = 768


def simple_call(kernel, name, operands, shapes, scalars=0, scratch=()):
    return pl.pallas_call(
        kernel,
        in_specs=[pl.BlockSpec(memory_space=pltpu.SMEM)] * scalars
        + [pl.BlockSpec(memory_space=pltpu.VMEM)] * (len(operands) - scalars),
        out_specs=[pl.BlockSpec(memory_space=pltpu.VMEM)] * len(shapes),
        out_shape=[jax.ShapeDtypeStruct(shape, kind) for shape, kind in shapes],
        scratch_shapes=[pltpu.VMEM(shape, FULL) for shape in scratch],
        compiler_params=pltpu.CompilerParams(vmem_limit_bytes=24 * 1024 * 1024),
        name=name,
    )(*operands)


SMALL = (32, 32, 96, 32, 32, 32, 128, 32)
EDGES = [sum(SMALL[:i]) for i in range(len(SMALL) + 1)]


def choose_columns(joint_weight, up_weight):
    c = lax.axis_index("ctx")
    k = lax.axis_index("core")
    (chosen,) = simple_call(
        choose_kernel,
        "choose_columns",
        (jnp.stack([c, k]), joint_weight, up_weight),
        [((2, 32, 3 * LOCAL + FEED), LOW)],
        1,
    )
    return in_order(k, chosen[0], shift(chosen[1], "core", 1), 0)


def fetch_layer(block, tokens, small, output_weight, down_weight):
    c = lax.axis_index("ctx")
    k = lax.axis_index("core")
    quarter = 2 * c + k
    down = lax.dynamic_slice_in_dim(down_weight, c * 64, 64, 0)
    block = jnp.concatenate([block, down], 1)
    weights = lax.all_gather(block, ("y", "x"), axis=0, tiled=True)
    vectors = jnp.concatenate(small + (jnp.zeros((512 - sum(SMALL),), LOW),)).reshape(4, 128)
    vectors = jnp.concatenate([vectors, jnp.zeros((28, 128), LOW)], 0)
    mixed = pair(after(jnp.concatenate([output_weight, vectors], 1), block), "core", 0)
    others, (got,) = together(direct_blocks(mixed, "x"), [shift(tokens[0], "ctx", 1)])
    later, got = lax.optimization_barrier((tokens[1], got))
    inputs = in_order(c, tokens[0], got, 1)
    mixed = stack_four(mixed, others, "x")
    out = lax.dynamic_index_in_dim(mixed, quarter, 0, False)[:, :D]
    vectors = mixed[:, :, D:].reshape(4, 2, 32, 128)[:, :, :8].reshape(64, 128)
    out = jnp.concatenate([out, vectors], 1)
    others, (inputs_other, got) = together(
        direct_blocks(out, "y"), [shift(inputs, "core", 1), shift(later, "ctx", 1)]
    )
    cotangent = in_order(c, later, got, 1)
    out = stack_four(out, others, "y")
    inputs = (inputs, inputs_other)
    cotangent = (cotangent, shift(cotangent, "core", 1))
    vectors = out[:, :, D:].reshape(32, 8, 128)[:, :4].reshape(32, 512)
    small = [vectors[:, a:b].reshape(-1).astype(FULL) for a, b in zip(EDGES, EDGES[1:])]
    joint_bias = lax.dynamic_index_in_dim(
        small[2].reshape(3, 4, 4, HEAD_DIM), quarter, 2, False
    ).reshape(-1)
    up_bias = small[6].reshape(16, 2, 2, HEAD_DIM)
    up_bias = lax.dynamic_index_in_dim(
        lax.dynamic_index_in_dim(up_bias, c, 2, False), k, 1, False
    ).reshape(-1)
    params = jnp.stack(
        [
            small[0],
            small[1],
            small[4],
            small[5],
            jnp.pad(joint_bias, (0, D - 3 * LOCAL)),
            up_bias,
            small[3] + small[7],
            jnp.zeros((D,), FULL),
        ]
    )
    layer = (params, weights, out.reshape(LOCAL, D + 128))
    return layer, inputs, cotangent


def return_layer(one, two, down, sums, beside, late):
    c = lax.axis_index("ctx")
    k = lax.axis_index("core")
    x = lax.axis_index("x")
    y = lax.axis_index("y")
    one = one.reshape(4, 4, 64, -1)
    two = two.reshape(4, 4, 64, -1)
    sums = sums + shift_pair(sums, "y", 1)
    ones, twos, (more, beside, core) = together(
        ring_start(one, "y", 0),
        ring_start(two, "x", 1),
        [shift_pair(sums, "y", 2), beside, late[1]],
    )
    sums = sums + more
    own, give = halves_of(late[0], core)
    ones, twos, (more, got) = together(
        ring_next(one, "y", 0, *ones),
        ring_next(two, "x", 1, *twos),
        [shift_pair(sums, "x", 1), shift(give, "ctx", 1)],
    )
    sums = sums + more
    one = plus(quarter_of(one, 0, y), *ones)
    two = plus(quarter_of(two, 1, x), *twos)
    out = one[:, :, SPLIT :].transpose(1, 0, 2).reshape(1, 64, D)
    out = jnp.where(
        jnp.arange(4)[:, None, None] == 2 * c + k, out, jnp.zeros_like(out)
    )
    one = jnp.concatenate([one[:, :, : SPLIT], out], -1)
    ones, twos, (more,) = together(
        direct(one, "x", 0), direct(two, "y", 0), [shift_pair(sums, "x", 2)]
    )
    sums = sums + more
    one = plus(quarter_of(one, 0, x), *ones)
    two = plus(quarter_of(two, 0, y), *twos)
    both = jnp.concatenate([one[:, :SPLIT], two, one[:, SPLIT:]], 1)
    both = both.reshape(2, 32, -1)
    width = FEED + 3 * LOCAL
    mine = take(both, k, 0)
    (other,), (more,) = together(
        [shift(take(both, 1 - k, 0), "core", 1)], [shift(sums, "core", 1)]
    )
    sums = in_order(k, sums[None], more[None], 0)
    block = in_order(k, mine[:, :width], other[:, :width], 0)
    out = plus(mine[:, width:], other[:, width:])
    (block_more, out_more, sums_more, down_more), _ = together(
        [shift(item, "ctx", 1) for item in (block, out, sums, down)], [beside]
    )
    place = (4 * y + x) * 2 + k
    vectors = [((1, width), FULL) for width in SMALL]
    joint, out, up, down, *vectors = simple_call(
        finish_kernel,
        "finish",
        (
            place[None],
            in_order(c, block[None], block_more[None], 0),
            in_order(c, down[None], down_more[None], 0),
            out,
            out_more,
            in_order(c, sums, sums_more, 0),
        ),
        [((1, 32, 3 * D), FULL), ((1, 32, D), FULL), ((1, 32, 4 * D), FULL), ((1, 128, D), FULL)]
        + vectors,
        1,
        ((8, D), (8, 4 * D), (8, 3 * D + 128)),
    )
    return joint, out, up, down, vectors, beside, own + got.astype(FULL)


def plus_full(left, right):
    return left.astype(FULL) + right.astype(FULL)


def take(block, index, dim):
    return lax.dynamic_index_in_dim(block, index, dim, False)


def halves_of(mine, other):
    c = lax.axis_index("ctx")
    total = plus_full(mine, other)
    total = total.reshape(total.shape[:-2] + (2, SEQ // 2, D))
    dim = total.ndim - 3
    return take(total, c, dim), take(total, 1 - c, dim).astype(LOW)


def sum_cores(mine, other):
    return halves_of(mine, shift(other, "core", 1))


def send_on(block):
    same = lax.ppermute(block, ("section", "ctx"), [(i, (i + 2) % 4) for i in range(4)])
    flip = lax.ppermute(block, ("section", "ctx"), [(i, 3 - i) for i in range(4)])
    return same, flip


def join(keep, whole, same, flip):
    mine = jnp.where(keep, whole, in_order(lax.axis_index("ctx"), same, flip, 0))
    return mine, shift(mine, "core", 1)


def split_two(results):
    return results[0], results[1], results[2:]


def shards(
    inputs,
    cotangent,
    segments,
    positions,
    attention_gain,
    attention_bias,
    joint_weight,
    joint_bias,
    output_weight,
    output_bias,
    feed_gain,
    feed_bias,
    up_weight,
    up_bias,
    down_weight,
    down_bias,
):
    section = lax.axis_index("section")
    count = inputs.shape[0]
    block = choose_columns(joint_weight[0], up_weight[0])
    pos = pair(after(positions[:, 0], block), "ctx", 1)
    pos = jnp.stack([pos, shift(pos, "core", 1)], 1)
    seg = after(segments[:, 0], block)
    seg = jnp.stack([seg, shift(seg, "core", 1)], 1)
    early, pos, seg = lax.optimization_barrier((inputs[:, 0], pos, seg))
    layer, whole_in, whole_grad = fetch_layer(
        block,
        (early, cotangent[:, 0]),
        (
            attention_gain[0],
            attention_bias[0],
            joint_bias[0],
            output_bias[0],
            feed_gain[0],
            feed_bias[0],
            up_bias[0],
            down_bias[0],
        ),
        output_weight[0],
        down_weight[0],
    )
    bias = layer[0][6]
    lane = jnp.arange(128) % HEAD_DIM
    rates = jnp.where(lane < ROT, 10000.0 ** (-2.0 * (lane % (ROT // 2)).astype(FULL) / ROT), 0.0)
    angle = pos.astype(FULL)[..., None] * rates
    cosine = jnp.cos(angle).reshape(count, TOKENS, 128)
    sine = (jnp.sin(angle) * jnp.where(lane < ROT // 2, -1.0, 1.0)).reshape(count, TOKENS, 128)
    places = [(seg[m][:, None, :], seg[m][:, :, None], cosine[m], sine[m]) for m in range(count)]
    c = lax.axis_index("ctx")

    def of(pair_, m):
        return tuple(item[m] for item in pair_)

    def own_tokens(whole):
        return take(whole.reshape(2, SEQ // 2, D), c, 0).astype(FULL)

    def over_ctx(base, own, give):
        return (base + own + shift(give, "ctx", 1).astype(FULL)).astype(LOW)

    own_in = inputs[:, 0].astype(FULL) + bias
    part = forward(of(whole_in, 0), places[0], layer, False)
    own, give = sum_cores(*part)
    a, b = of(whole_in, 1)
    part = forward((after(a, give), b), places[1], layer, False)
    result = over_ctx(own_in[0], own, give)
    sent = [send_on(result)]
    own, give = sum_cores(part[0], after(part[1], result))
    result = over_ctx(own_in[1], own, give)
    sent.append(send_on(result))
    own_grad = cotangent[:, 0].astype(FULL)
    same, flip, _ = lax.optimization_barrier((*sent[0], result))
    hidden = [join(section == 0, whole_in[0][0], same, flip)]
    *out_zero, saved_zero = split_two(forward(hidden[0], places[0], layer, True))
    part = backward(of(whole_grad, 0), hidden[0], places[0], layer, saved_zero, False)
    own, give = sum_cores(*part)
    same, flip, _ = lax.optimization_barrier((*sent[1], part[0]))
    a, b = join(section == 0, whole_in[0][1], same, flip)
    hidden.append((a, after(b, give)))
    *out_one, saved_one = split_two(forward(hidden[1], places[1], layer, True))
    got = after(shift(give, "ctx", 1), out_one[0])
    result = (own_grad[0] + own + got.astype(FULL)).astype(LOW)
    sent = [send_on(result)]
    a, b = of(whole_grad, 1)
    part = backward((after(a, result), b), hidden[1], places[1], layer, saved_one, False)
    same, flip, *part = lax.optimization_barrier((*sent[0], *part))
    a, b = join(section == 1, whole_grad[0][0], same, flip)
    own, give = sum_cores(*part)
    result = over_ctx(own_grad[1], own, give)
    sent.append(send_on(result))
    saved = [saved_zero, saved_one]
    grads = [(a, after(b, result))]

    def last(m):
        return backward(grads[m], hidden[m], places[m], layer, saved[m], True, m == 1)

    *part_zero, up_zero, joint_zero, sums_zero = last(0)
    same, flip, part_zero[0] = lax.optimization_barrier((*sent[1], part_zero[0]))
    grads.append(join(section == 1, whole_grad[0][1], same, flip))
    both = (*grads[0], *grads[1])
    (down,) = call(
        down_kernel,
        "down_gradient",
        ((saved_zero[7], saved_one[7]), both),
        [((FEED, D), LOW)],
        None,
    )
    down_share = lax.psum_scatter(down, ("y", "x"), scatter_dimension=0, tiled=True)
    ready = grads[1][1]
    outs = [
        jnp.stack([out_zero[i], out_one[i], after(part_zero[i], ready)]) for i in range(2)
    ]
    grads[1] = (grads[1][0], after(grads[1][1], down))
    *part_one, up_one, joint_one, sums_one = last(1)
    own_early, give = sum_cores(*outs)
    one, two = own_call(
        weights_kernel,
        "weight_gradients",
        (
            (saved_zero[1], saved_one[1]),
            (up_zero, up_one),
            (saved_zero[6], saved_one[6]),
            (after(both[0], give), *both[1:]),
            (saved_zero[0], saved_one[0]),
            (joint_zero, joint_one),
        ),
        [((D, SPLIT + LOCAL), LOW), ((D, FEED - SPLIT + 3 * LOCAL), LOW)],
        None,
        2,
    )
    joint_grad, out_grad, up_grad, down_grad, small, got, late = return_layer(
        one,
        two,
        down_share,
        sums_zero + sums_one,
        shift(give, "ctx", 1),
        (part_one[0], shift(part_one[1], "core", 1)),
    )
    base = jnp.stack(
        [own_tokens(hidden[0][0]) + bias, own_tokens(hidden[1][0]) + bias, own_tokens(grads[0][0])]
    )
    early = (base + own_early + got.astype(FULL)).astype(LOW)
    late = (own_tokens(grads[1][0])[None] + late).astype(LOW)
    section_out = early[None, :2, None]
    input_grad = jnp.concatenate([early[2:], late])[None, :, None]
    return (
        section_out,
        input_grad,
        small[0],
        small[1],
        joint_grad,
        small[2],
        out_grad,
        small[3],
        small[4],
        small[5],
        up_grad,
        small[6],
        down_grad,
        small[7],
    )


def solution(mesh):
    finer = Mesh(mesh.devices.reshape(2, 2, 4, 4, 2), ("section", "ctx", "y", "x", "core"))
    fsdp = ("y", "x", "core")
    vector = P("section", fsdp)
    matrix = P("section", fsdp, None)
    tokens = P(None, fsdp, "ctx", None)
    kept = P("section", None, fsdp, "ctx", None)
    params = (
        vector,
        vector,
        matrix,
        vector,
        matrix,
        vector,
        vector,
        vector,
        matrix,
        vector,
        matrix,
        vector,
    )
    return jax.shard_map(
        shards,
        mesh=finer,
        in_specs=(tokens, tokens, P(None, fsdp, None), P(None, fsdp, "ctx")) + params,
        out_specs=(kept, kept) + params,
        check_vma=False,
    )
```
